32 devices in a mesh: tm: 8 (over z, x), space: 4 (over y, core).
Axes of the slice: x: 2, y: 2, z: 4, core: 2. Of those that a mesh axis runs over, the one named last changes fastest.
Arguments:
- guess: float32 [8, 1024, 1024], P('tm', 'space'), may hold values from -2.5 to 2.5
- kappa: float32 [1024, 1024], P('space'), may hold values from 0.25 to 1
- rate: float32 [1024, 1024], P('space'), may hold values from 0.005 to 0.02
Outputs:
- c_points: float32 [8, 1024, 1024], P('tm', 'space')
- last_fine: float32 [8, 1024, 1024], P('tm', 'space')
The draws below stay inside these ranges and needn't reach their ends.
All inputs are finite; a program needn't handle non-finite values.
Results may differ from the reference program's by a relative error of at most 0.00002.
Values sent between devices are 32-bit elements; how exact they have to be, the bound alone decides.
A program may use at most 64 MiB of HBM per device.

```python
import math
import jax
import jax.numpy as jnp

NY = 1024
STEPS = 4
GROUP = 4
SWEEPS = 2
NT = 8
NX = 1024


def level_of(key, dims, cuts, smallest, top_value):
    loudness, own = 1.0, jax.random.fold_in(key, 6)
    for axis_at, blocks in cuts:
        heights = jnp.exp(jax.random.uniform(jax.random.fold_in(own, axis_at), (blocks,), jnp.float32, smallest / len(cuts), top_value / len(cuts)))
        loudness = loudness * jnp.repeat(heights, dims[axis_at] // blocks).reshape([-1 if axis == axis_at else 1 for axis in range(len(dims))])
    return loudness


def bell_draw(own_key, extent, scale, most, cuts=(), kind=jnp.bfloat16):
    result = scale * jax.random.normal(own_key, extent, jnp.float32)
    if cuts:
        result = result * level_of(own_key, extent, cuts, -0.22, 0.18)
    return jnp.clip(result, -most, most).astype(kind)


def setup_inputs(seed: int = 0) -> dict:
    arg_keys = jax.random.split(jax.random.key(seed), 4)
    return {
        "guess": bell_draw(arg_keys[0], (NT, NX, NY), 0.5, 2.5, ((0, 8), (1, 4)), jnp.float32),
        "kappa": jnp.clip(jnp.exp(math.log(1.0) - 1.3862944 * jax.random.uniform(arg_keys[1], (NX, NY), jnp.float32) ** level_of(arg_keys[1], (NX, NY), ((0, 4),), -0.2, 0.2)), 0.25, 1.0),
        "rate": jnp.clip(jnp.exp(math.log(0.02) - 1.3862944 * jax.random.uniform(arg_keys[2], (NX, NY), jnp.float32) ** level_of(arg_keys[2], (NX, NY), ((0, 4),), -0.2, 0.2)), 0.005, 0.02),
    }


DIFFUSION = 0.05


def advance_padded(padded, kappa, rate, scale):
    centre = padded[..., 1:-1, 1:-1]
    laplace = padded[..., 2:, 1:-1] + padded[..., :-2, 1:-1] + padded[..., 1:-1, 2:] + padded[..., 1:-1, :-2] - 4.0 * centre
    return centre + scale * (DIFFUSION * kappa * laplace + rate * (centre - centre * centre * centre))


def advance(state, kappa, rate, scale):
    widths = [(0, 0)] * (state.ndim - 2) + [(1, 1), (1, 1)]
    return advance_padded(jnp.pad(state, widths), kappa, rate, scale)


def propagate(state, kappa, rate, count):
    for repeat in range(count):
        state = advance(state, kappa, rate, 1.0)
    return state


def reference(guess, kappa, rate):
    first = guess[:1]
    relaxed = jnp.concatenate([first, propagate(guess[:-1], kappa, rate, STEPS)], axis=0)
    earlier = relaxed[:-1]
    fine_image = propagate(earlier, kappa, rate, STEPS)
    coarse_image = advance(earlier, kappa, rate, float(STEPS))
    defect = jnp.concatenate([jnp.zeros_like(first), fine_image - coarse_image], axis=0)
    groups = NT // GROUP
    coarse = relaxed.reshape(groups, GROUP, NX, NY)
    defects = defect.reshape(groups, GROUP, NX, NY)
    for sweep_number in range(SWEEPS):
        for member in range(1, GROUP):
            coarse = coarse.at[:, member].set(advance(coarse[:, member - 1], kappa, rate, float(STEPS)) + defects[:, member])
        coarse = coarse.at[1:, 0].set(advance(coarse[:-1, GROUP - 1], kappa, rate, float(STEPS)) + defects[1:, 0])
    c_points = coarse.reshape(NT, NX, NY)
    last_fine = propagate(c_points, kappa, rate, STEPS - 1)
    return c_points, last_fine
```

```python
import functools
import jax
import jax.numpy as jnp
from jax import lax
from jax.experimental import pallas as pl
from jax.experimental.pallas import tpu as pltpu
from jax.sharding import PartitionSpec as P

STEPS = 4
GROUP = 4
SWEEPS = 2


DIFFUSION = 0.05
PAD = 8
CHUNK = 16
MESH = pl.DeviceIdType.MESH


def step_rows(src, kw, rw, low, count, shift, scale, cols):
    band = src[pl.ds(pl.multiple_of(low - PAD, 8), count + 2 * PAD), :]
    centre = band[PAD : PAD + count]
    above = band[PAD - 1 : PAD - 1 + count]
    below = band[PAD + 1 : PAD + 1 + count]
    width = centre.shape[1]
    left = jnp.where(cols == 0, 0.0, pltpu.roll(centre, 1, 1))
    right = jnp.where(cols == width - 1, 0.0, pltpu.roll(centre, width - 1, 1))
    where = pl.ds(pl.multiple_of(low + shift, 8), count)
    laplace = (above + below) + (left + right) - 4.0 * centre
    change = kw[where, :] * laplace + rw[where, :] * (centre - centre * centre * centre)
    return centre + (change if scale == 1.0 else scale * change)


def kernel(
    points, strips, guess, kappa, rate, c_out, f_out,
    kw, rw, ga, gb, x_ref, ya, yb, z_ref, da, db, cr, vo, ve, vw, u1, u2, kh,
    k_send, k_recv, g_send, g_recv, c_send, c_recv, f_send, f_recv,
):
    rows, width = kappa.shape
    half = rows // 2
    wide = ga.shape[0]
    halo = (wide - 2 * PAD - half) // 2
    chunks = (wide - 2 * PAD) // CHUNK
    skipped = halo // CHUNK
    full = vw.shape[0]
    pairs = points // 2
    tm, s = lax.axis_index("tm"), lax.axis_index("space")
    p, b = tm // 2, tm % 2
    coarse_scale = float(STEPS)
    cols = lax.broadcasted_iota(jnp.int32, (CHUNK, width), 1)
    shift = b * half
    partner = p * 2 + (1 - b)

    later, earlier = p < pairs - 1, p > 0
    below, above = s < strips - 1, s > 0
    even, odd = b == 0, b == 1

    targets = [
        (below, (tm, s + 1)), (above, (tm, s - 1)), (s >= 0, (partner, s)),
        (even & above, (tm + 1, s - 1)), (later, (tm + 2, s)),
        (odd & later, (tm + 1, s)), (odd & later & below, (tm + 1, s + 1)),
        (odd & later & above, (tm + 2, s - 1)),
    ]
    sources = [
        (below, (tm, s + 1)), (above, (tm, s - 1)), (s >= 0, (partner, s)),
        (odd & below, (tm - 1, s + 1)), (earlier, (tm - 2, s)),
        (even & earlier, (tm - 1, s)), (even & earlier & above, (tm - 1, s - 1)),
        (odd & earlier & below, (tm - 2, s + 1)),
    ]
    barrier = pltpu.get_barrier_semaphore()
    for condition, device in sources:
        @pl.when(condition)
        def _(device=device):
            pl.semaphore_signal(barrier, inc=1, device_id=device, device_id_type=MESH)
    count = sum(condition.astype(jnp.int32) for condition, _ in targets)
    pl.semaphore_wait(barrier, count)

    def copy(src, dst, send, recv, device):
        return pltpu.make_async_remote_copy(
            src_ref=src, dst_ref=dst, send_sem=send, recv_sem=recv,
            device_id=device, device_id_type=MESH,
        )

    main = half + halo
    first, last = pl.ds(0, halo), pl.ds(rows - halo, halo)
    upper, lower = pl.ds(PAD, halo), pl.ds(PAD + main, halo)
    main_even, main_odd = pl.ds(PAD + halo, main), pl.ds(PAD, main)
    head, tail = pl.ds(0, main), pl.ds(rows - main, main)
    halves = [
        (below, copy(kappa.at[last], kh.at[0], k_send.at[0], k_recv.at[0], (tm, s + 1))),
        (below, copy(rate.at[last], kh.at[1], k_send.at[1], k_recv.at[1], (tm, s + 1))),
        (above, copy(kappa.at[first], kh.at[2], k_send.at[2], k_recv.at[2], (tm, s - 1))),
        (above, copy(rate.at[first], kh.at[3], k_send.at[3], k_recv.at[3], (tm, s - 1))),
    ]
    own = guess.at[0]
    fields = [
        (even & below, copy(own.at[last], gb.at[upper], g_send.at[0], g_recv.at[0], (tm, s + 1))),
        (even & above, copy(own.at[first], gb.at[lower], g_send.at[1], g_recv.at[0], (tm + 1, s - 1))),
        (odd & later & below, copy(own.at[last], ga.at[upper], g_send.at[0], g_recv.at[2], (tm + 1, s + 1))),
        (odd & later & above, copy(own.at[first], ga.at[lower], g_send.at[1], g_recv.at[2], (tm + 2, s - 1))),
        (even, copy(own.at[tail], gb.at[main_odd], g_send.at[2], g_recv.at[1], (partner, s))),
        (odd & later, copy(own.at[tail], ga.at[main_odd], g_send.at[2], g_recv.at[3], (tm + 2, s))),
        (odd & later, copy(own.at[head], ga.at[main_even], g_send.at[3], g_recv.at[3], (tm + 1, s))),
    ]
    for condition, transfer in halves + fields:
        @pl.when(condition)
        def _(transfer=transfer):
            transfer.start()

    zeros = jnp.zeros((PAD, width), jnp.float32)
    for ref in (ga, gb, x_ref, ya, yb, z_ref, cr, vo, vw, u1, u2, kw, rw):
        ref[pl.ds(0, PAD), :] = zeros
        ref[pl.ds(ref.shape[0] - PAD, PAD), :] = zeros
    blank = jnp.zeros((halo, width), jnp.float32)

    def fill(index, carry):
        start = pl.multiple_of(index * CHUNK, CHUNK)
        at = pl.multiple_of(start + PAD + halo, 8)
        kw[pl.ds(at, CHUNK), :] = DIFFUSION * kappa[pl.ds(start, CHUNK), :]
        rw[pl.ds(at, CHUNK), :] = rate[pl.ds(start, CHUNK), :]
        return carry

    lax.fori_loop(0, rows // CHUNK, fill, 0)

    @pl.when(even)
    def _():
        def place(index, carry):
            start = pl.multiple_of(index * CHUNK, CHUNK)
            at = pl.multiple_of(start + PAD + halo, 8)
            gb[pl.ds(at, CHUNK), :] = guess[0, pl.ds(start, CHUNK), :]
            return carry

        lax.fori_loop(0, main // CHUNK, place, 0)

    @pl.when(even & ~above)
    def _():
        ga[upper, :] = blank
        gb[upper, :] = blank

    @pl.when(odd & ~below)
    def _():
        ga[lower, :] = blank
        gb[lower, :] = blank

    end = pl.ds(full - PAD - halo, halo)

    @pl.when(above)
    def _():
        halves[0][1].wait_recv()
        halves[1][1].wait_recv()
        kw[upper, :] = DIFFUSION * kh[0]
        rw[upper, :] = kh[1]

    @pl.when(~above)
    def _():
        kw[upper, :] = blank
        rw[upper, :] = blank

    @pl.when(below)
    def _():
        halves[2][1].wait_recv()
        halves[3][1].wait_recv()
        kw[end, :] = DIFFUSION * kh[2]
        rw[end, :] = kh[3]

    @pl.when(~below)
    def _():
        kw[end, :] = blank
        rw[end, :] = blank

    def chunk(index):
        return pl.ds(pl.multiple_of(index * CHUNK + PAD, 8), CHUNK)

    def advance(src, index, scale):
        return step_rows(src, kw, rw, index * CHUNK + PAD, CHUNK, shift, scale, cols)

    def sweep(src, dst):
        def body(index, carry):
            dst[chunk(index), :] = advance(src, index, 1.0)
            return carry

        lax.fori_loop(0, chunks, body, 0)

    def march(src, scratch, dst, times):
        for turn in range(times):
            out = dst if (times - 1 - turn) % 2 == 0 else scratch
            sweep(src, out)
            src = out

    def defects(field, relaxed, out, whole):
        march(field, x_ref, relaxed, STEPS)
        march(relaxed, z_ref, x_ref, STEPS - 1)

        def body(index, carry):
            fine = advance(x_ref, index, 1.0)
            coarse = advance(relaxed, index, coarse_scale)
            out[chunk(index), :] = jnp.where(whole, fine, fine - coarse)
            return carry

        lax.fori_loop(0, chunks, body, 0)

    @pl.when(even & above)
    def _():
        fields[0][1].wait_recv()

    @pl.when(odd & below)
    def _():
        fields[1][1].wait_recv()

    @pl.when(odd)
    def _():
        fields[4][1].wait_recv()

    defects(gb, yb, db, p == 0)

    @pl.when(earlier)
    def _():
        @pl.when(even & above)
        def _():
            fields[2][1].wait_recv()

        @pl.when(odd & below)
        def _():
            fields[3][1].wait_recv()

        @pl.when(even)
        def _():
            fields[6][1].wait_recv()

        @pl.when(odd)
        def _():
            fields[5][1].wait_recv()

        defects(ga, ya, da, p < 0)

    def chain(index):
        part = chunk(index)
        return copy(ve.at[part], cr.at[part], c_send.at[index], c_recv.at[index], (tm + 2, s))

    def target(index, side):
        return pl.ds(pl.multiple_of(index * CHUNK + PAD + side * half, 8), CHUNK)

    kept = chunks - skipped

    def forward(index, src):
        return copy(
            src.at[chunk(index)], vw.at[target(index, b)], f_send.at[index], f_recv.at[index],
            (partner, s),
        )

    def hand_over(index):
        @pl.when(even & (index < kept))
        def _():
            forward(index, vo).start()
            vw[target(index, 0), :] = cr[chunk(index), :]

        @pl.when(odd & (index >= skipped))
        def _():
            forward(index, cr).start()
            vw[target(index, 1), :] = vo[chunk(index), :]

    @pl.when(p == 0)
    def _():
        def body(index, carry):
            part = chunk(index)
            ve[part, :] = db[part, :]
            chain(index).start()
            vo[part, :] = yb[part, :]
            cr[part, :] = gb[part, :]
            hand_over(index)
            return carry

        lax.fori_loop(0, chunks, body, 0)

    @pl.when(earlier)
    def _():
        def body(index, carry):
            @pl.when(index < chunks)
            def _():
                chain(index).wait_recv()

            @pl.when((index >= 1) & (index <= chunks))
            def _():
                now = index - 1
                vo[chunk(now), :] = advance(cr, now, coarse_scale) + da[chunk(now), :]

            @pl.when((index >= 2) & later)
            def _():
                now = index - 2
                ve[chunk(now), :] = advance(vo, now, coarse_scale) + db[chunk(now), :]
                chain(now).start()

            @pl.when((index >= 1) & (index <= chunks))
            def _():
                hand_over(index - 1)

            return carry

        lax.fori_loop(0, chunks + 2, body, 0)

    def collect(index, carry):
        forward(index + skipped * (1 - b), vo).wait_recv()
        return carry

    lax.fori_loop(0, kept, collect, 0)

    def wide_step(src, dst, low, offset, blocks):
        def body(index, carry):
            start = index * CHUNK + low
            out = pl.ds(pl.multiple_of(start - offset, 8), CHUNK)
            dst[out, :] = step_rows(src, kw, rw, start, CHUNK, 0, 1.0, cols)
            return carry

        lax.fori_loop(0, blocks, body, 0)

    src = vw
    for turn in range(STEPS - 2):
        out = u1 if turn % 2 == 0 else u2
        wide_step(src, out, PAD, 0, (full - 2 * PAD) // CHUNK)
        src = out

    def finish(index, carry):
        start = index * CHUNK
        low = start + PAD + halo
        out = pl.ds(pl.multiple_of(start, CHUNK), CHUNK)
        f_out[0, out, :] = step_rows(src, kw, rw, low, CHUNK, 0, 1.0, cols)
        c_out[0, out, :] = vw[pl.ds(pl.multiple_of(low, 8), CHUNK), :]
        return carry

    lax.fori_loop(0, rows // CHUNK, finish, 0)

    for condition, transfer in halves + fields:
        @pl.when(condition)
        def _(transfer=transfer):
            transfer.wait_send()

    @pl.when(later)
    def _():
        def body(index, carry):
            chain(index).wait_send()
            return carry

        lax.fori_loop(0, chunks, body, 0)

    def sent(index, carry):
        forward(index + skipped * b, vo).wait_send()
        return carry

    lax.fori_loop(0, kept, sent, 0)


def chained(points, strips, guess, kappa, rate):
    rows, width = kappa.shape
    halo = halo_of(points)
    wide = rows // 2 + 2 * halo + 2 * PAD
    full = rows + 2 * halo + 2 * PAD
    chunks = (wide - 2 * PAD) // CHUNK
    f32 = jnp.float32
    part, whole = pltpu.VMEM((wide, width), f32), pltpu.VMEM((full, width), f32)
    dma = pltpu.SemaphoreType.DMA
    vmem = pl.BlockSpec(memory_space=pltpu.VMEM)
    return pl.pallas_call(
        functools.partial(kernel, points, strips),
        out_shape=[jax.ShapeDtypeStruct(guess.shape, f32)] * 2,
        in_specs=[vmem] * 3,
        out_specs=[vmem] * 2,
        scratch_shapes=[whole, whole] + [part] * 11 + [whole] * 3
        + [pltpu.VMEM((4, halo, width), f32)]
        + [dma((4,))] * 4 + [dma((chunks,))] * 4,
        compiler_params=pltpu.CompilerParams(
            collective_id=0, has_side_effects=True, vmem_limit_bytes=48 * 2**20
        ),
    )(guess, kappa, rate)


def halo_of(points):
    needed = 2 * STEPS + max(points - 3, 0) + STEPS - 1
    return -(-needed // CHUNK) * CHUNK


def extended(shard, sides, width):
    for axis, dim in sides:
        peers, length = (lax.axis_size(axis), shard.shape[dim])
        up = [(i, (i + 1) % peers) for i in range(peers - 1)]
        down = [(j, i) for i, j in up]
        last = lax.slice_in_dim(shard, length - width, length, axis=dim)
        initial = lax.slice_in_dim(shard, 0, width, axis=dim)
        before = lax.ppermute(last, axis, up)
        after = lax.ppermute(initial, axis, down)
        shard = jnp.concatenate([before, shard, after], axis=dim)
    return shard


def from_behind(value, axis, steps):
    count = lax.axis_size(axis)
    initial, last = (max(0, -steps), min(count, count - steps))
    return lax.ppermute(value, axis, [(source, source + steps) for source in range(initial, last)])


def advance_padded(padded, kappa, rate, scale):
    centre = padded[1:-1, 1:-1]
    laplace = (
        padded[2:, 1:-1] + padded[:-2, 1:-1] + padded[1:-1, 2:] + padded[1:-1, :-2] - 4.0 * centre
    )
    return centre + scale * (
        DIFFUSION * kappa * laplace + rate * (centre - centre * centre * centre)
    )


def deep_border(state, count):
    return extended(state, (("space", 0),), count)


def deep_step(wide, margin, widened, scale):
    rows = widened.shape[1] - 2 * STEPS
    height = wide.shape[0] - 2
    lower = STEPS - (margin - 1)
    kappa_rows = widened[0, lower : lower + height]
    rate_rows = widened[1, lower : lower + height]
    stepped = advance_padded(jnp.pad(wide, ((0, 0), (1, 1))), kappa_rows, rate_rows, scale)
    strip = lax.axis_index("space")
    total = rows * lax.axis_size("space")
    global_rows = strip * rows - (margin - 1) + lax.broadcasted_iota(jnp.int32, stepped.shape, 0)
    inside = (global_rows >= 0) & (global_rows < total)
    return jnp.where(inside, stepped, jnp.zeros_like(stepped))


def deep_march(wide, margin, widened, count):
    for repeat in range(count):
        wide = deep_step(wide, margin, widened, 1.0)
        margin = margin - 1
    return wide


def forward(state):
    return from_behind(state, "tm", 1)


def local(guess, kappa, rate):
    position = lax.axis_index("tm")
    member = position % GROUP
    coarse_scale = float(STEPS)
    state = guess[0]
    incoming = forward(state)
    widened = extended(jnp.stack([kappa, rate]), (("space", 1),), STEPS)
    marched = deep_march(deep_border(incoming, STEPS), STEPS, widened, STEPS)
    relaxed = jnp.where(position == 0, state, marched)
    incoming = forward(relaxed)
    wide = deep_border(incoming, STEPS)
    rows = relaxed.shape[0]
    band = jnp.pad(wide[STEPS - 1 : STEPS + rows + 1], ((0, 0), (1, 1)))
    coarse_image = advance_padded(band, kappa, rate, coarse_scale)
    fine_image = deep_march(wide, STEPS, widened, STEPS)
    defect = jnp.where(position == 0, jnp.zeros_like(fine_image), fine_image - coarse_image)
    coarse = relaxed
    for sweep_number in range(SWEEPS):
        for turn in range(GROUP):
            arrived = from_behind(coarse, "tm", 1)
            framed = extended(arrived, (("space", 0),), 1)
            framed = jnp.pad(framed, ((0, 0), (1, 1)))
            updated = advance_padded(framed, kappa, rate, coarse_scale) + defect
            if turn + 1 < GROUP:
                active = member == turn + 1
            else:
                active = (member == 0) & (position >= GROUP)
            coarse = jnp.where(active, updated, coarse)
    last_fine = deep_march(deep_border(coarse, STEPS - 1), STEPS - 1, widened, STEPS - 1)
    return (coarse[None], last_fine[None])


def solution(mesh):
    points, strips = mesh.shape["tm"], mesh.shape["space"]

    def run(guess, kappa, rate):
        half = kappa.shape[0] // 2
        settled = points <= GROUP * SWEEPS and points % 2 == 0 and points >= 4
        if settled and half % CHUNK == 0 and halo_of(points) <= half:
            return tuple(chained(points, strips, guess, kappa, rate))
        return local(guess, kappa, rate)

    return jax.shard_map(
        run,
        mesh=mesh,
        in_specs=(P("tm", "space", None), P("space", None), P("space", None)),
        out_specs=(P("tm", "space", None), P("tm", "space", None)),
        check_vma=False,
    )
```

```python
import functools
import jax
import jax.numpy as jnp
from jax import lax
from jax.experimental import pallas as pl
from jax.experimental.pallas import tpu as pltpu
from jax.sharding import PartitionSpec as P

STEPS = 4
GROUP = 4
SWEEPS = 2


DIFFUSION = 0.05
PAD = 8
CHUNK = 8
LANES = 128
MESH = pl.DeviceIdType.MESH


def block_of(rows):
    return max(size for size in range(8, min(rows, 136) + 1, 8) if rows % size == 0)


def kernel(
    points, strips, guess, kappa, rate, c_out, f_out,
    kw, rw, aw, ga, gb, x_ref, ya, yb, z_ref, w_ref, da, db, cr, vo, ve, vw, u1, u2,
    local_sem, k_send, k_recv, g_send, g_recv, c_send, c_recv, f_send, f_recv,
):
    rows, width = kappa.shape
    tiles = width // LANES
    half = rows // 2
    wide = ga.shape[1]
    full = vw.shape[1]
    halo = (wide - 2 * PAD - half) // 2
    margin = halo - 2 * STEPS
    chunks = (half + 2 * margin) // CHUNK
    skipped = margin // CHUNK
    kept = chunks - skipped
    pairs = points // 2
    tm, s = lax.axis_index("tm"), lax.axis_index("space")
    p, b = tm // 2, tm % 2
    coarse_scale = float(STEPS)
    shift = b * half
    partner = p * 2 + (1 - b)

    later, earlier = p < pairs - 1, p > 0
    below, above = s < strips - 1, s > 0
    even, odd = b == 0, b == 1

    targets = [
        (below, (tm, s + 1)), (above, (tm, s - 1)), (s >= 0, (partner, s)),
        (even & above, (tm + 1, s - 1)), (later, (tm + 2, s)),
        (odd & later, (tm + 1, s)), (odd & later & below, (tm + 1, s + 1)),
        (odd & later & above, (tm + 2, s - 1)),
    ]
    sources = [
        (below, (tm, s + 1)), (above, (tm, s - 1)), (s >= 0, (partner, s)),
        (odd & below, (tm - 1, s + 1)), (earlier, (tm - 2, s)),
        (even & earlier, (tm - 1, s)), (even & earlier & above, (tm - 1, s - 1)),
        (odd & earlier & below, (tm - 2, s + 1)),
    ]
    barrier = pltpu.get_barrier_semaphore()
    for condition, device in sources:
        @pl.when(condition)
        def _(device=device):
            pl.semaphore_signal(barrier, inc=1, device_id=device, device_id_type=MESH)

    main = half + halo
    first, last = (0, halo), (rows - halo, halo)
    head, tail = (0, main), (rows - main, main)
    upper, lower = pl.ds(PAD, halo), pl.ds(PAD + main, halo)
    main_even, main_odd = pl.ds(PAD + halo, main), pl.ds(PAD, main)
    end = pl.ds(PAD + halo + rows, halo)
    middle = pl.ds(PAD + halo, rows)
    own = guess.at[0]

    def columns(src, part):
        start, count = part
        return [src.at[pl.ds(start, count), pl.ds(t * LANES, LANES)] for t in range(tiles)]

    def fetch(src, part, dst, place, sem):
        def start():
            for t, column in enumerate(columns(src, part)):
                pltpu.make_async_copy(column, dst.at[t, place], sem).start()

        def wait():
            pltpu.make_async_copy(dst.at[:, place], dst.at[:, place], sem).wait()

        return start, wait

    def copy(src, dst, send, recv, device):
        return pltpu.make_async_remote_copy(
            src_ref=src, dst_ref=dst, send_sem=send, recv_sem=recv,
            device_id=device, device_id_type=MESH,
        )

    class Send:
        def __init__(self, src, part, dst, place, send, recv, device):
            self.start_all = [
                copy(column, dst.at[t, place], send, recv, device)
                for t, column in enumerate(columns(src, part))
            ]
            self.whole = copy(dst.at[:, place], dst.at[:, place], send, recv, device)

        def start(self):
            for one in self.start_all:
                one.start()

        def wait_recv(self):
            self.whole.wait_recv()

        def wait_send(self):
            self.whole.wait_send()

    k_local = fetch(kappa, (0, rows), kw, middle, local_sem.at[0])
    r_local = fetch(rate, (0, rows), rw, middle, local_sem.at[1])
    g_local = fetch(own, head, gb, main_even, local_sem.at[2])
    k_local[0]()
    r_local[0]()

    @pl.when(even)
    def _():
        g_local[0]()

    sends = [
        (below, Send(kappa, last, kw, upper, k_send.at[0], k_recv.at[0], (tm, s + 1))),
        (below, Send(rate, last, rw, upper, k_send.at[1], k_recv.at[1], (tm, s + 1))),
        (above, Send(kappa, first, kw, end, k_send.at[2], k_recv.at[2], (tm, s - 1))),
        (above, Send(rate, first, rw, end, k_send.at[3], k_recv.at[3], (tm, s - 1))),
        (even & below, Send(own, last, gb, upper, g_send.at[0], g_recv.at[0], (tm, s + 1))),
        (even & above, Send(own, first, gb, lower, g_send.at[1], g_recv.at[0], (tm + 1, s - 1))),
        (odd & later & below, Send(own, last, ga, upper, g_send.at[0], g_recv.at[2], (tm + 1, s + 1))),
        (odd & later & above, Send(own, first, ga, lower, g_send.at[1], g_recv.at[2], (tm + 2, s - 1))),
        (even, Send(own, tail, gb, main_odd, g_send.at[2], g_recv.at[1], (partner, s))),
        (odd & later, Send(own, tail, ga, main_odd, g_send.at[2], g_recv.at[3], (tm + 2, s))),
        (odd & later, Send(own, head, ga, main_even, g_send.at[3], g_recv.at[3], (tm + 1, s))),
    ]
    halves, fields = sends[:4], sends[4:]
    count = sum(condition.astype(jnp.int32) for condition, _ in targets)
    pl.semaphore_wait(barrier, count)
    for condition, transfer in sends:
        @pl.when(condition)
        def _(transfer=transfer):
            transfer.start()

    zeros = jnp.zeros((tiles, PAD, LANES), jnp.float32)
    for ref in (ga, gb, x_ref, ya, yb, z_ref, w_ref, cr, vo, vw, u1, u2):
        ref[:, pl.ds(0, PAD), :] = zeros
        ref[:, pl.ds(ref.shape[1] - PAD, PAD), :] = zeros
    rim = jnp.zeros((tiles, 2 * STEPS, LANES), jnp.float32)
    for ref in (cr, vo):
        ref[:, pl.ds(PAD, 2 * STEPS), :] = rim
        ref[:, pl.ds(wide - PAD - 2 * STEPS, 2 * STEPS), :] = rim
    blank = jnp.zeros((tiles, halo, LANES), jnp.float32)

    @pl.when(even & ~above)
    def _():
        ga[:, upper, :] = blank
        gb[:, upper, :] = blank

    @pl.when(odd & ~below)
    def _():
        ga[:, lower, :] = blank
        gb[:, lower, :] = blank

    @pl.when(~above)
    def _():
        kw[:, upper, :] = blank
        rw[:, upper, :] = blank

    @pl.when(~below)
    def _():
        kw[:, end, :] = blank
        rw[:, end, :] = blank

    k_local[1]()
    r_local[1]()

    @pl.when(above)
    def _():
        halves[0][1].wait_recv()
        halves[1][1].wait_recv()

    @pl.when(below)
    def _():
        halves[2][1].wait_recv()
        halves[3][1].wait_recv()

    def scaled(index, carry):
        part = pl.ds(pl.multiple_of(index * 32 + PAD, 8), 32)
        k = DIFFUSION * kw[:, part, :]
        kw[:, part, :] = k
        aw[:, part, :] = (1.0 + rw[:, part, :]) - 4.0 * k
        return carry

    lax.fori_loop(0, (rows + 2 * halo) // 32, scaled, 0)

    def step(src, low, size, offset):
        lane = lax.broadcasted_iota(jnp.int32, (size, LANES), 1)
        at = pl.ds(pl.multiple_of(low + offset, 8), size)
        here = pl.ds(pl.multiple_of(low, 8), size)
        centres = [src[t, here, :] for t in range(tiles)]
        to_right = [pltpu.roll(centre, 1, 1) for centre in centres]
        to_left = [pltpu.roll(centre, LANES - 1, 1) for centre in centres]
        results = []
        for t, centre in enumerate(centres):
            before = to_right[t - 1] if t > 0 else 0.0
            after = to_left[t + 1] if t + 1 < tiles else 0.0
            left = jnp.where(lane == 0, before, to_right[t])
            right = jnp.where(lane == LANES - 1, after, to_left[t])
            beside = src[t, pl.ds(low - 1, size), :] + src[t, pl.ds(low + 1, size), :]
            total = beside + (left + right)
            own_part = centre * (aw[t, at, :] - rw[t, at, :] * (centre * centre))
            results.append(own_part + kw[t, at, :] * total)
        return results, centres

    block = block_of(wide - 2 * PAD)

    def sweep(src, dst):
        def body(index, carry):
            low = index * block + PAD
            results, _ = step(src, low, block, shift)
            for t, value in enumerate(results):
                dst[t, pl.ds(pl.multiple_of(low, 8), block), :] = value
            return carry

        lax.fori_loop(0, (wide - 2 * PAD) // block, body, 0)

    def march(src, scratch, dst, times):
        for turn in range(times):
            out = dst if (times - 1 - turn) % 2 == 0 else scratch
            sweep(src, out)
            src = out

    def defects(field, relaxed, out, weight):
        march(field, x_ref, relaxed, STEPS)
        sweep(relaxed, w_ref)
        march(w_ref, z_ref, x_ref, STEPS - 2)

        def body(index, carry):
            low = index * block + PAD
            here = pl.ds(pl.multiple_of(low, 8), block)
            results, _ = step(x_ref, low, block, shift)
            for t, fine in enumerate(results):
                coarse = coarse_scale * w_ref[t, here, :] - (coarse_scale - 1.0) * relaxed[t, here, :]
                out[t, here, :] = fine - weight * coarse
            return carry

        lax.fori_loop(0, (wide - 2 * PAD) // block, body, 0)

    @pl.when(later)
    def _():
        @pl.when(even)
        def _():
            g_local[1]()

        @pl.when(even & above)
        def _():
            fields[0][1].wait_recv()

        @pl.when(odd & below)
        def _():
            fields[1][1].wait_recv()

        @pl.when(odd)
        def _():
            fields[4][1].wait_recv()

        defects(gb, yb, db, jnp.where(p == 0, 0.0, 1.0))

    @pl.when(earlier)
    def _():
        @pl.when(even & above)
        def _():
            fields[2][1].wait_recv()

        @pl.when(odd & below)
        def _():
            fields[3][1].wait_recv()

        @pl.when(even)
        def _():
            fields[6][1].wait_recv()

        @pl.when(odd)
        def _():
            fields[5][1].wait_recv()

        defects(ga, ya, da, 1.0)

    base = PAD + 2 * STEPS

    def chunk(index):
        return pl.ds(pl.multiple_of(index * CHUNK + base, 8), CHUNK)

    def chain(index):
        part = chunk(index)
        return copy(ve.at[:, part], cr.at[:, part], c_send.at[index], c_recv.at[index], (tm + 2, s))

    def target(index, side):
        return pl.ds(pl.multiple_of(index * CHUNK + PAD + side * half, 8), CHUNK)

    def forward(index, src):
        return copy(
            src.at[:, chunk(index)], vw.at[:, target(index, b)], f_send.at[index], f_recv.at[index],
            (partner, s),
        )

    def hand_over(index):
        @pl.when(even & (index < kept))
        def _():
            forward(index, vo).start()
            vw[:, target(index, 0), :] = cr[:, chunk(index), :]

        @pl.when(odd & (index >= skipped))
        def _():
            forward(index, cr).start()
            vw[:, target(index, 1), :] = vo[:, chunk(index), :]

    def corrected(src, defect, out, index):
        here = chunk(index)
        results, centres = step(src, index * CHUNK + base, CHUNK, shift)
        for t, value in enumerate(results):
            image = coarse_scale * value - (coarse_scale - 1.0) * centres[t]
            out[t, here, :] = image + defect[t, here, :]

    @pl.when(p == 0)
    def _():
        def body(index, carry):
            part = chunk(index)
            ve[:, part, :] = db[:, part, :]
            chain(index).start()
            vo[:, part, :] = yb[:, part, :]
            cr[:, part, :] = gb[:, part, :]
            hand_over(index)
            return carry

        lax.fori_loop(0, chunks, body, 0)

    @pl.when(earlier)
    def _():
        def body(index, carry):
            @pl.when(index < chunks)
            def _():
                chain(index).wait_recv()

            @pl.when((index >= 1) & (index <= chunks))
            def _():
                corrected(cr, da, vo, index - 1)

            @pl.when((index >= 2) & later)
            def _():
                corrected(vo, db, ve, index - 2)
                chain(index - 2).start()

            @pl.when((index >= 1) & (index <= chunks))
            def _():
                hand_over(index - 1)

            return carry

        lax.fori_loop(0, chunks + 2, body, 0)

    def collect(index, carry):
        forward(index + skipped * (1 - b), vo).wait_recv()
        return carry

    lax.fori_loop(0, kept, collect, 0)

    offset = halo - margin
    size = block_of(full - 2 * PAD)
    src = vw
    for turn in range(STEPS - 2):
        out = u1 if turn % 2 == 0 else u2

        def body(index, carry, src=src, out=out):
            low = index * size + PAD
            results, _ = step(src, low, size, offset)
            for t, value in enumerate(results):
                out[t, pl.ds(pl.multiple_of(low, 8), size), :] = value
            return carry

        lax.fori_loop(0, (full - 2 * PAD) // size, body, 0)
        src = out
    size_out = block_of(rows)

    def finish(index, carry):
        start = index * size_out
        low = start + PAD + margin
        out = pl.ds(pl.multiple_of(start, 8), size_out)
        results, _ = step(src, low, size_out, offset)
        for t, value in enumerate(results):
            lanes = pl.ds(t * LANES, LANES)
            f_out[0, out, lanes] = value
            c_out[0, out, lanes] = vw[t, pl.ds(pl.multiple_of(low, 8), size_out), :]
        return carry

    lax.fori_loop(0, rows // size_out, finish, 0)

    @pl.when(~later & even)
    def _():
        g_local[1]()

    @pl.when(~later)
    def _():
        @pl.when(even & above)
        def _():
            fields[0][1].wait_recv()

        @pl.when(odd & below)
        def _():
            fields[1][1].wait_recv()

        @pl.when(odd)
        def _():
            fields[4][1].wait_recv()

    for condition, transfer in sends:
        @pl.when(condition)
        def _(transfer=transfer):
            transfer.wait_send()

    @pl.when(later)
    def _():
        def body(index, carry):
            chain(index).wait_send()
            return carry

        lax.fori_loop(0, chunks, body, 0)

    def sent(index, carry):
        forward(index + skipped * b, vo).wait_send()
        return carry

    lax.fori_loop(0, kept, sent, 0)


def halo_of(points):
    needed = 2 * STEPS + max(points - 3, 0) + STEPS - 1
    return -(-needed // CHUNK) * CHUNK


def chained(points, strips, guess, kappa, rate):
    rows, width = kappa.shape
    tiles = width // LANES
    halo = halo_of(points)
    margin = halo - 2 * STEPS
    wide = rows // 2 + 2 * halo + 2 * PAD
    full = rows + 2 * margin + 2 * PAD
    chunks = (rows // 2 + 2 * margin) // CHUNK
    f32 = jnp.float32

    def held(height):
        return pltpu.VMEM((tiles, height, LANES), f32)

    part, whole, coefficient = held(wide), held(full), held(rows + 2 * halo + 2 * PAD)
    dma = pltpu.SemaphoreType.DMA
    vmem = pl.BlockSpec(memory_space=pltpu.VMEM)
    anywhere = pl.BlockSpec(memory_space=pl.ANY)
    return pl.pallas_call(
        functools.partial(kernel, points, strips),
        out_shape=[jax.ShapeDtypeStruct(guess.shape, f32)] * 2,
        in_specs=[anywhere] * 3,
        out_specs=[vmem] * 2,
        scratch_shapes=[coefficient] * 3 + [part] * 12 + [whole] * 3
        + [dma((3,))] + [dma((4,))] * 4 + [dma((chunks,))] * 4,
        compiler_params=pltpu.CompilerParams(
            collective_id=0, has_side_effects=True, vmem_limit_bytes=48 * 2**20
        ),
    )(guess, kappa, rate)


def extended(shard, sides, width):
    for axis, dim in sides:
        peers, length = (lax.axis_size(axis), shard.shape[dim])
        up = [(i, (i + 1) % peers) for i in range(peers - 1)]
        down = [(j, i) for i, j in up]
        last = lax.slice_in_dim(shard, length - width, length, axis=dim)
        initial = lax.slice_in_dim(shard, 0, width, axis=dim)
        before = lax.ppermute(last, axis, up)
        after = lax.ppermute(initial, axis, down)
        shard = jnp.concatenate([before, shard, after], axis=dim)
    return shard


def from_behind(value, axis, steps):
    count = lax.axis_size(axis)
    initial, last = (max(0, -steps), min(count, count - steps))
    return lax.ppermute(value, axis, [(source, source + steps) for source in range(initial, last)])


def advance_padded(padded, kappa, rate, scale):
    centre = padded[1:-1, 1:-1]
    laplace = (
        padded[2:, 1:-1] + padded[:-2, 1:-1] + padded[1:-1, 2:] + padded[1:-1, :-2] - 4.0 * centre
    )
    return centre + scale * (
        DIFFUSION * kappa * laplace + rate * (centre - centre * centre * centre)
    )


def deep_border(state, count):
    return extended(state, (("space", 0),), count)


def deep_step(wide, margin, widened, scale):
    rows = widened.shape[1] - 2 * STEPS
    height = wide.shape[0] - 2
    lower = STEPS - (margin - 1)
    kappa_rows = widened[0, lower : lower + height]
    rate_rows = widened[1, lower : lower + height]
    stepped = advance_padded(jnp.pad(wide, ((0, 0), (1, 1))), kappa_rows, rate_rows, scale)
    strip = lax.axis_index("space")
    total = rows * lax.axis_size("space")
    global_rows = strip * rows - (margin - 1) + lax.broadcasted_iota(jnp.int32, stepped.shape, 0)
    inside = (global_rows >= 0) & (global_rows < total)
    return jnp.where(inside, stepped, jnp.zeros_like(stepped))


def deep_march(wide, margin, widened, count):
    for repeat in range(count):
        wide = deep_step(wide, margin, widened, 1.0)
        margin = margin - 1
    return wide


def forward(state):
    return from_behind(state, "tm", 1)


def local(guess, kappa, rate):
    position = lax.axis_index("tm")
    member = position % GROUP
    coarse_scale = float(STEPS)
    state = guess[0]
    incoming = forward(state)
    widened = extended(jnp.stack([kappa, rate]), (("space", 1),), STEPS)
    marched = deep_march(deep_border(incoming, STEPS), STEPS, widened, STEPS)
    relaxed = jnp.where(position == 0, state, marched)
    incoming = forward(relaxed)
    wide = deep_border(incoming, STEPS)
    rows = relaxed.shape[0]
    band = jnp.pad(wide[STEPS - 1 : STEPS + rows + 1], ((0, 0), (1, 1)))
    coarse_image = advance_padded(band, kappa, rate, coarse_scale)
    fine_image = deep_march(wide, STEPS, widened, STEPS)
    defect = jnp.where(position == 0, jnp.zeros_like(fine_image), fine_image - coarse_image)
    coarse = relaxed
    for sweep_number in range(SWEEPS):
        for turn in range(GROUP):
            arrived = from_behind(coarse, "tm", 1)
            framed = extended(arrived, (("space", 0),), 1)
            framed = jnp.pad(framed, ((0, 0), (1, 1)))
            updated = advance_padded(framed, kappa, rate, coarse_scale) + defect
            if turn + 1 < GROUP:
                active = member == turn + 1
            else:
                active = (member == 0) & (position >= GROUP)
            coarse = jnp.where(active, updated, coarse)
    last_fine = deep_march(deep_border(coarse, STEPS - 1), STEPS - 1, widened, STEPS - 1)
    return (coarse[None], last_fine[None])


def solution(mesh):
    points, strips = mesh.shape["tm"], mesh.shape["space"]

    def run(guess, kappa, rate):
        rows, width = kappa.shape
        settled = points <= GROUP * SWEEPS and points % 2 == 0 and points >= 4
        aligned = rows % 32 == 0 and width % LANES == 0 and (2 * STEPS) % 8 == 0
        if settled and aligned and halo_of(points) % 16 == 0 and 2 * halo_of(points) <= rows:
            return tuple(chained(points, strips, guess, kappa, rate))
        return local(guess, kappa, rate)

    return jax.shard_map(
        run,
        mesh=mesh,
        in_specs=(P("tm", "space", None), P("space", None), P("space", None)),
        out_specs=(P("tm", "space", None), P("tm", "space", None)),
        check_vma=False,
    )
```

```python
import functools
import jax
import jax.numpy as jnp
from jax import lax
from jax.experimental import pallas as pl
from jax.experimental.pallas import tpu as pltpu
from jax.sharding import PartitionSpec as P

STEPS = 4
GROUP = 4
SWEEPS = 2


DIFFUSION = 0.05
PAD = 8
CHUNK = 8
LANES = 128
MESH = pl.DeviceIdType.MESH


def block_of(rows):
    return max(size for size in range(8, min(rows, 32) + 1, 8) if rows % size == 0)


def kernel(
    points, strips, guess, kappa, rate, c_out, f_out,
    kw, rw, aw, ga, gb, x_ref, ya, yb, z_ref, w_ref, da, db, cr, vo, ve, vw, u1, u2,
    local_sem, k_send, k_recv, g_send, g_recv, c_send, c_recv, f_send, f_recv,
):
    rows, width = kappa.shape
    tiles = width // LANES
    half = rows // 2
    wide = ga.shape[1]
    full = vw.shape[1]
    halo = (wide - 2 * PAD - half) // 2
    margin = halo - 2 * STEPS
    chunks = (half + 2 * margin) // CHUNK
    skipped = margin // CHUNK
    kept = chunks - skipped
    pairs = points // 2
    tm, s = lax.axis_index("tm"), lax.axis_index("space")
    p, b = tm // 2, tm % 2
    coarse_scale = float(STEPS)
    shift = b * half
    partner = p * 2 + (1 - b)

    later, earlier = p < pairs - 1, p > 0
    below, above = s < strips - 1, s > 0
    even, odd = b == 0, b == 1

    targets = [
        (below, (tm, s + 1)), (above, (tm, s - 1)), (s >= 0, (partner, s)),
        (even & above, (tm + 1, s - 1)), (later, (tm + 2, s)),
        (odd & later, (tm + 1, s)), (odd & later & below, (tm + 1, s + 1)),
        (odd & later & above, (tm + 2, s - 1)),
    ]
    sources = [
        (below, (tm, s + 1)), (above, (tm, s - 1)), (s >= 0, (partner, s)),
        (odd & below, (tm - 1, s + 1)), (earlier, (tm - 2, s)),
        (even & earlier, (tm - 1, s)), (even & earlier & above, (tm - 1, s - 1)),
        (odd & earlier & below, (tm - 2, s + 1)),
    ]
    barrier = pltpu.get_barrier_semaphore()
    for condition, device in sources:
        @pl.when(condition)
        def _(device=device):
            pl.semaphore_signal(barrier, inc=1, device_id=device, device_id_type=MESH)

    main = half + halo
    first, last = (0, halo), (rows - halo, halo)
    head, tail = (0, main), (rows - main, main)
    upper, lower = pl.ds(PAD, halo), pl.ds(PAD + main, halo)
    main_even, main_odd = pl.ds(PAD + halo, main), pl.ds(PAD, main)
    end = pl.ds(PAD + halo + rows, halo)
    middle = pl.ds(PAD + halo, rows)
    own = guess.at[0]

    def columns(src, part):
        start, count = part
        return [src.at[pl.ds(start, count), pl.ds(t * LANES, LANES)] for t in range(tiles)]

    def fetch(src, part, dst, place, sem):
        def start():
            for t, column in enumerate(columns(src, part)):
                pltpu.make_async_copy(column, dst.at[t, place], sem).start()

        def wait():
            pltpu.make_async_copy(dst.at[:, place], dst.at[:, place], sem).wait()

        return start, wait

    def copy(src, dst, send, recv, device):
        return pltpu.make_async_remote_copy(
            src_ref=src, dst_ref=dst, send_sem=send, recv_sem=recv,
            device_id=device, device_id_type=MESH,
        )

    class Send:
        def __init__(self, src, part, dst, place, send, recv, device):
            self.start_all = [
                copy(column, dst.at[t, place], send, recv, device)
                for t, column in enumerate(columns(src, part))
            ]
            self.whole = copy(dst.at[:, place], dst.at[:, place], send, recv, device)

        def start(self):
            for one in self.start_all:
                one.start()

        def wait_recv(self):
            self.whole.wait_recv()

        def wait_send(self):
            self.whole.wait_send()

    k_local = fetch(kappa, (0, rows), kw, middle, local_sem.at[0])
    r_local = fetch(rate, (0, rows), rw, middle, local_sem.at[1])
    g_local = fetch(own, head, gb, main_even, local_sem.at[2])
    k_local[0]()
    r_local[0]()

    @pl.when(even)
    def _():
        g_local[0]()

    sends = [
        (below, Send(kappa, last, kw, upper, k_send.at[0], k_recv.at[0], (tm, s + 1))),
        (below, Send(rate, last, rw, upper, k_send.at[1], k_recv.at[1], (tm, s + 1))),
        (above, Send(kappa, first, kw, end, k_send.at[2], k_recv.at[2], (tm, s - 1))),
        (above, Send(rate, first, rw, end, k_send.at[3], k_recv.at[3], (tm, s - 1))),
        (even & below, Send(own, last, gb, upper, g_send.at[0], g_recv.at[0], (tm, s + 1))),
        (even & above, Send(own, first, gb, lower, g_send.at[1], g_recv.at[0], (tm + 1, s - 1))),
        (odd & later & below, Send(own, last, ga, upper, g_send.at[0], g_recv.at[2], (tm + 1, s + 1))),
        (odd & later & above, Send(own, first, ga, lower, g_send.at[1], g_recv.at[2], (tm + 2, s - 1))),
        (even, Send(own, tail, gb, main_odd, g_send.at[2], g_recv.at[1], (partner, s))),
        (odd & later, Send(own, tail, ga, main_odd, g_send.at[2], g_recv.at[3], (tm + 2, s))),
        (odd & later, Send(own, head, ga, main_even, g_send.at[3], g_recv.at[3], (tm + 1, s))),
    ]
    halves, fields = sends[:4], sends[4:]
    count = sum(condition.astype(jnp.int32) for condition, _ in targets)
    pl.semaphore_wait(barrier, count)
    for condition, transfer in sends:
        @pl.when(condition)
        def _(transfer=transfer):
            transfer.start()

    zeros = jnp.zeros((tiles, PAD, LANES), jnp.float32)
    for ref in (ga, gb, x_ref, ya, yb, z_ref, w_ref, cr, vo, vw, u1, u2):
        ref[:, pl.ds(0, PAD), :] = zeros
        ref[:, pl.ds(ref.shape[1] - PAD, PAD), :] = zeros
    rim = jnp.zeros((tiles, 2 * STEPS, LANES), jnp.float32)
    for ref in (cr, vo):
        ref[:, pl.ds(PAD, 2 * STEPS), :] = rim
        ref[:, pl.ds(wide - PAD - 2 * STEPS, 2 * STEPS), :] = rim
    blank = jnp.zeros((tiles, halo, LANES), jnp.float32)

    @pl.when(even & ~above)
    def _():
        ga[:, upper, :] = blank
        gb[:, upper, :] = blank

    @pl.when(odd & ~below)
    def _():
        ga[:, lower, :] = blank
        gb[:, lower, :] = blank

    @pl.when(~above)
    def _():
        kw[:, upper, :] = blank
        rw[:, upper, :] = blank

    @pl.when(~below)
    def _():
        kw[:, end, :] = blank
        rw[:, end, :] = blank

    k_local[1]()
    r_local[1]()

    @pl.when(above)
    def _():
        halves[0][1].wait_recv()
        halves[1][1].wait_recv()

    @pl.when(below)
    def _():
        halves[2][1].wait_recv()
        halves[3][1].wait_recv()

    def scaled(index, carry):
        part = pl.ds(pl.multiple_of(index * 32 + PAD, 8), 32)
        k = DIFFUSION * kw[:, part, :]
        kw[:, part, :] = k
        aw[:, part, :] = (1.0 + rw[:, part, :]) - 4.0 * k
        return carry

    lax.fori_loop(0, (rows + 2 * halo) // 32, scaled, 0)

    def step(src, low, size, offset, emit):
        lane = lax.broadcasted_iota(jnp.int32, (size, LANES), 1)
        at = pl.ds(pl.multiple_of(low + offset, 8), size)
        here = pl.ds(pl.multiple_of(low, 8), size)
        centre = src[0, here, :]
        before = after = 0.0
        to_left = pltpu.roll(centre, LANES - 1, 1)
        for t in range(tiles):
            to_right = pltpu.roll(centre, 1, 1)
            if t + 1 < tiles:
                following = src[t + 1, here, :]
                after = pltpu.roll(following, LANES - 1, 1)
            else:
                following, after = None, 0.0
            left = jnp.where(lane == 0, before, to_right)
            right = jnp.where(lane == LANES - 1, after, to_left)
            beside = src[t, pl.ds(low - 1, size), :] + src[t, pl.ds(low + 1, size), :]
            total = beside + (left + right)
            own_part = centre * (aw[t, at, :] - rw[t, at, :] * (centre * centre))
            emit(t, own_part + kw[t, at, :] * total, centre)
            before, centre, to_left = to_right, following, after

    def over(start, stop, act):
        size = block_of(stop - start)
        count = (stop - start) // size

        def body(index, carry):
            act(index * size + start, size)
            return carry

        lax.fori_loop(0, count, body, 0, unroll=True)

    def sweep(src, dst, start=PAD, stop=wide - PAD, offset=shift):
        def act(low, size):
            def emit(t, value, centre):
                dst[t, pl.ds(pl.multiple_of(low, 8), size), :] = value

            step(src, low, size, offset, emit)

        over(start, stop, act)

    def march(src, scratch, dst, times):
        for turn in range(times):
            out = dst if (times - 1 - turn) % 2 == 0 else scratch
            sweep(src, out)
            src = out

    def defects(field, relaxed, out, weight):
        march(field, x_ref, relaxed, STEPS)
        sweep(relaxed, w_ref)
        march(w_ref, z_ref, x_ref, STEPS - 2)

        def act(low, size):
            here = pl.ds(pl.multiple_of(low, 8), size)

            def emit(t, fine, centre):
                coarse = coarse_scale * w_ref[t, here, :] - (coarse_scale - 1.0) * relaxed[t, here, :]
                out[t, here, :] = fine - weight * coarse

            step(x_ref, low, size, shift, emit)

        over(PAD, wide - PAD, act)

    @pl.when(later)
    def _():
        @pl.when(even)
        def _():
            g_local[1]()

        @pl.when(even & above)
        def _():
            fields[0][1].wait_recv()

        @pl.when(odd & below)
        def _():
            fields[1][1].wait_recv()

        @pl.when(odd)
        def _():
            fields[4][1].wait_recv()

        defects(gb, yb, db, jnp.where(p == 0, 0.0, 1.0))

    @pl.when(earlier)
    def _():
        @pl.when(even & above)
        def _():
            fields[2][1].wait_recv()

        @pl.when(odd & below)
        def _():
            fields[3][1].wait_recv()

        @pl.when(even)
        def _():
            fields[6][1].wait_recv()

        @pl.when(odd)
        def _():
            fields[5][1].wait_recv()

        defects(ga, ya, da, 1.0)

    base = PAD + 2 * STEPS

    def chunk(index):
        return pl.ds(pl.multiple_of(index * CHUNK + base, 8), CHUNK)

    def chain(index):
        part = chunk(index)
        return copy(ve.at[:, part], cr.at[:, part], c_send.at[index], c_recv.at[index], (tm + 2, s))

    def target(index, side):
        return pl.ds(pl.multiple_of(index * CHUNK + PAD + side * half, 8), CHUNK)

    def forward(index, src):
        return copy(
            src.at[:, chunk(index)], vw.at[:, target(index, b)], f_send.at[index], f_recv.at[index],
            (partner, s),
        )

    def hand_over(index):
        @pl.when(even & (index < kept))
        def _():
            forward(index, vo).start()
            vw[:, target(index, 0), :] = cr[:, chunk(index), :]

        @pl.when(odd & (index >= skipped))
        def _():
            forward(index, cr).start()
            vw[:, target(index, 1), :] = vo[:, chunk(index), :]

    def corrected(src, defect, out, index):
        here = chunk(index)

        def emit(t, value, centre):
            image = coarse_scale * value - (coarse_scale - 1.0) * centre
            out[t, here, :] = image + defect[t, here, :]

        step(src, index * CHUNK + base, CHUNK, shift, emit)

    @pl.when(p == 0)
    def _():
        def body(index, carry):
            part = chunk(index)
            ve[:, part, :] = db[:, part, :]
            chain(index).start()
            vo[:, part, :] = yb[:, part, :]
            cr[:, part, :] = gb[:, part, :]
            hand_over(index)
            return carry

        lax.fori_loop(0, chunks, body, 0)

    @pl.when(earlier)
    def _():
        def body(index, carry):
            @pl.when(index < chunks)
            def _():
                chain(index).wait_recv()

            @pl.when((index >= 1) & (index <= chunks))
            def _():
                corrected(cr, da, vo, index - 1)

            @pl.when((index >= 2) & later)
            def _():
                corrected(vo, db, ve, index - 2)
                chain(index - 2).start()

            @pl.when((index >= 1) & (index <= chunks))
            def _():
                hand_over(index - 1)

            return carry

        lax.fori_loop(0, chunks + 2, body, 0)

    def collect(index, carry):
        forward(index + skipped * (1 - b), vo).wait_recv()
        return carry

    lax.fori_loop(0, kept, collect, 0)

    offset = halo - margin
    src = vw
    for turn in range(STEPS - 2):
        out = u1 if turn % 2 == 0 else u2
        sweep(src, out, PAD, full - PAD, offset)
        src = out

    def finish(low, size):
        out = pl.ds(pl.multiple_of(low - PAD - margin, 8), size)

        def emit(t, value, centre):
            lanes = pl.ds(t * LANES, LANES)
            f_out[0, out, lanes] = value
            c_out[0, out, lanes] = vw[t, pl.ds(pl.multiple_of(low, 8), size), :]

        step(src, low, size, offset, emit)

    over(PAD + margin, PAD + margin + rows, finish)

    @pl.when(~later & even)
    def _():
        g_local[1]()

    @pl.when(~later)
    def _():
        @pl.when(even & above)
        def _():
            fields[0][1].wait_recv()

        @pl.when(odd & below)
        def _():
            fields[1][1].wait_recv()

        @pl.when(odd)
        def _():
            fields[4][1].wait_recv()

    for condition, transfer in sends:
        @pl.when(condition)
        def _(transfer=transfer):
            transfer.wait_send()

    @pl.when(later)
    def _():
        def body(index, carry):
            chain(index).wait_send()
            return carry

        lax.fori_loop(0, chunks, body, 0)

    def sent(index, carry):
        forward(index + skipped * b, vo).wait_send()
        return carry

    lax.fori_loop(0, kept, sent, 0)


def halo_of(points):
    needed = 2 * STEPS + max(points - 3, 0) + STEPS - 1
    return -(-needed // CHUNK) * CHUNK


def chained(points, strips, guess, kappa, rate):
    rows, width = kappa.shape
    tiles = width // LANES
    halo = halo_of(points)
    margin = halo - 2 * STEPS
    wide = rows // 2 + 2 * halo + 2 * PAD
    full = rows + 2 * margin + 2 * PAD
    chunks = (rows // 2 + 2 * margin) // CHUNK
    f32 = jnp.float32

    def held(height):
        return pltpu.VMEM((tiles, height, LANES), f32)

    part, whole, coefficient = held(wide), held(full), held(rows + 2 * halo + 2 * PAD)
    dma = pltpu.SemaphoreType.DMA
    vmem = pl.BlockSpec(memory_space=pltpu.VMEM)
    anywhere = pl.BlockSpec(memory_space=pltpu.HBM)
    return pl.pallas_call(
        functools.partial(kernel, points, strips),
        out_shape=[jax.ShapeDtypeStruct(guess.shape, f32)] * 2,
        in_specs=[anywhere] * 3,
        out_specs=[vmem] * 2,
        scratch_shapes=[coefficient] * 3 + [part] * 12 + [whole] * 3
        + [dma((3,))] + [dma((4,))] * 4 + [dma((chunks,))] * 4,
        compiler_params=pltpu.CompilerParams(
            collective_id=0, has_side_effects=True, vmem_limit_bytes=63 * 2**20
        ),
    )(guess, kappa, rate)


def extended(shard, sides, width):
    for axis, dim in sides:
        peers, length = (lax.axis_size(axis), shard.shape[dim])
        up = [(i, (i + 1) % peers) for i in range(peers - 1)]
        down = [(j, i) for i, j in up]
        last = lax.slice_in_dim(shard, length - width, length, axis=dim)
        initial = lax.slice_in_dim(shard, 0, width, axis=dim)
        before = lax.ppermute(last, axis, up)
        after = lax.ppermute(initial, axis, down)
        shard = jnp.concatenate([before, shard, after], axis=dim)
    return shard


def from_behind(value, axis, steps):
    count = lax.axis_size(axis)
    initial, last = (max(0, -steps), min(count, count - steps))
    return lax.ppermute(value, axis, [(source, source + steps) for source in range(initial, last)])


def advance_padded(padded, kappa, rate, scale):
    centre = padded[1:-1, 1:-1]
    laplace = (
        padded[2:, 1:-1] + padded[:-2, 1:-1] + padded[1:-1, 2:] + padded[1:-1, :-2] - 4.0 * centre
    )
    return centre + scale * (
        DIFFUSION * kappa * laplace + rate * (centre - centre * centre * centre)
    )


def deep_border(state, count):
    return extended(state, (("space", 0),), count)


def deep_step(wide, margin, widened, scale):
    rows = widened.shape[1] - 2 * STEPS
    height = wide.shape[0] - 2
    lower = STEPS - (margin - 1)
    kappa_rows = widened[0, lower : lower + height]
    rate_rows = widened[1, lower : lower + height]
    stepped = advance_padded(jnp.pad(wide, ((0, 0), (1, 1))), kappa_rows, rate_rows, scale)
    strip = lax.axis_index("space")
    total = rows * lax.axis_size("space")
    global_rows = strip * rows - (margin - 1) + lax.broadcasted_iota(jnp.int32, stepped.shape, 0)
    inside = (global_rows >= 0) & (global_rows < total)
    return jnp.where(inside, stepped, jnp.zeros_like(stepped))


def deep_march(wide, margin, widened, count):
    for repeat in range(count):
        wide = deep_step(wide, margin, widened, 1.0)
        margin = margin - 1
    return wide


def forward(state):
    return from_behind(state, "tm", 1)


def local(guess, kappa, rate):
    position = lax.axis_index("tm")
    member = position % GROUP
    coarse_scale = float(STEPS)
    state = guess[0]
    incoming = forward(state)
    widened = extended(jnp.stack([kappa, rate]), (("space", 1),), STEPS)
    marched = deep_march(deep_border(incoming, STEPS), STEPS, widened, STEPS)
    relaxed = jnp.where(position == 0, state, marched)
    incoming = forward(relaxed)
    wide = deep_border(incoming, STEPS)
    rows = relaxed.shape[0]
    band = jnp.pad(wide[STEPS - 1 : STEPS + rows + 1], ((0, 0), (1, 1)))
    coarse_image = advance_padded(band, kappa, rate, coarse_scale)
    fine_image = deep_march(wide, STEPS, widened, STEPS)
    defect = jnp.where(position == 0, jnp.zeros_like(fine_image), fine_image - coarse_image)
    coarse = relaxed
    for sweep_number in range(SWEEPS):
        for turn in range(GROUP):
            arrived = from_behind(coarse, "tm", 1)
            framed = extended(arrived, (("space", 0),), 1)
            framed = jnp.pad(framed, ((0, 0), (1, 1)))
            updated = advance_padded(framed, kappa, rate, coarse_scale) + defect
            if turn + 1 < GROUP:
                active = member == turn + 1
            else:
                active = (member == 0) & (position >= GROUP)
            coarse = jnp.where(active, updated, coarse)
    last_fine = deep_march(deep_border(coarse, STEPS - 1), STEPS - 1, widened, STEPS - 1)
    return (coarse[None], last_fine[None])


def solution(mesh):
    points, strips = mesh.shape["tm"], mesh.shape["space"]

    def run(guess, kappa, rate):
        rows, width = kappa.shape
        settled = points <= GROUP * SWEEPS and points % 2 == 0 and points >= 4
        aligned = rows % 32 == 0 and width % LANES == 0 and (2 * STEPS) % 8 == 0
        if settled and aligned and halo_of(points) % 16 == 0 and 2 * halo_of(points) <= rows:
            return tuple(chained(points, strips, guess, kappa, rate))
        return local(guess, kappa, rate)

    return jax.shard_map(
        run,
        mesh=mesh,
        in_specs=(P("tm", "space", None), P("space", None), P("space", None)),
        out_specs=(P("tm", "space", None), P("tm", "space", None)),
        check_vma=False,
    )
```

```python
import functools
import jax
import jax.numpy as jnp
from jax import lax
from jax.experimental import pallas as pl
from jax.experimental.pallas import tpu as pltpu
from jax.sharding import PartitionSpec as P

STEPS = 4
GROUP = 4
SWEEPS = 2


DIFFUSION = 0.05
PAD = 8
CHUNK = 8
PIECES = 6
LANES = 128
MESH = pl.DeviceIdType.MESH


def block_of(rows):
    return max(size for size in range(8, min(rows, 32) + 1, 8) if rows % size == 0)


def kernel(
    points, strips, guess, kappa, rate, c_out, f_out,
    kw, rw, aw, ga, gb, x_ref, ya, yb, z_ref, w_ref, da, db, cr, vo, ve, vw, u1, u2, st,
    local_sem, k_send, k_recv, g_send, g_recv, c_send, c_recv, f_send, f_recv,
    t_send, t_recv, o_send, o_recv,
):
    rows, width = kappa.shape
    tiles = width // LANES
    half = rows // 2
    wide = ga.shape[1]
    full = vw.shape[1]
    halo = (wide - 2 * PAD - half) // 2
    margin = halo - 2 * STEPS
    chunks = (half + 2 * margin) // CHUNK
    skipped = margin // CHUNK
    kept = chunks - skipped
    pairs = points // 2
    tm, s = lax.axis_index("tm"), lax.axis_index("space")
    p, b = tm // 2, tm % 2
    coarse_scale = float(STEPS)
    shift = b * half
    partner = p * 2 + (1 - b)

    later, earlier = p < pairs - 1, p > 0
    below, above = s < strips - 1, s > 0
    even, odd = b == 0, b == 1

    targets = [
        (below, (tm, s + 1)), (above, (tm, s - 1)), (s >= 0, (partner, s)),
        (even & above, (tm + 1, s - 1)), (later, (tm + 2, s)),
        (odd & later & below, (tm + 1, s + 1)),
        (odd & later & above, (tm + 2, s - 1)),
    ]
    sources = [
        (below, (tm, s + 1)), (above, (tm, s - 1)), (s >= 0, (partner, s)),
        (odd & below, (tm - 1, s + 1)), (earlier, (tm - 2, s)),
        (even & earlier & above, (tm - 1, s - 1)),
        (odd & earlier & below, (tm - 2, s + 1)),
    ]
    barrier = pltpu.get_barrier_semaphore()
    for condition, device in sources:
        @pl.when(condition)
        def _(device=device):
            pl.semaphore_signal(barrier, inc=1, device_id=device, device_id_type=MESH)

    main = half + halo
    first, last = (0, halo), (rows - halo, halo)
    head, tail = (0, main), (rows - main, main)
    upper, lower = pl.ds(PAD, halo), pl.ds(PAD + main, halo)
    main_even, main_odd = pl.ds(PAD + halo, main), pl.ds(PAD, main)
    end = pl.ds(PAD + halo + rows, halo)
    middle = pl.ds(PAD + halo, rows)
    own = guess.at[0]

    def columns(src, part):
        start, count = part
        return [src.at[pl.ds(start, count), pl.ds(t * LANES, LANES)] for t in range(tiles)]

    def fetch(src, part, dst, place, sem):
        def start():
            for t, column in enumerate(columns(src, part)):
                pltpu.make_async_copy(column, dst.at[t, place], sem).start()

        def wait():
            pltpu.make_async_copy(dst.at[:, place], dst.at[:, place], sem).wait()

        return start, wait

    def copy(src, dst, send, recv, device):
        return pltpu.make_async_remote_copy(
            src_ref=src, dst_ref=dst, send_sem=send, recv_sem=recv,
            device_id=device, device_id_type=MESH,
        )

    class Send:
        def __init__(self, src, part, dst, place, send, recv, device):
            self.start_all = [
                copy(column, dst.at[t, place], send, recv, device)
                for t, column in enumerate(columns(src, part))
            ]
            self.whole = copy(dst.at[:, place], dst.at[:, place], send, recv, device)

        def start(self):
            for one in self.start_all:
                one.start()

        def wait_recv(self):
            self.whole.wait_recv()

        def wait_send(self):
            self.whole.wait_send()

    k_local = fetch(kappa, (0, rows), kw, middle, local_sem.at[0])
    r_local = fetch(rate, (0, rows), rw, middle, local_sem.at[1])
    g_local = fetch(own, head, gb, main_even, local_sem.at[2])
    k_local[0]()
    r_local[0]()

    @pl.when(even)
    def _():
        g_local[0]()

    sends = [
        (below, Send(kappa, last, kw, upper, k_send.at[0], k_recv.at[0], (tm, s + 1))),
        (below, Send(rate, last, rw, upper, k_send.at[1], k_recv.at[1], (tm, s + 1))),
        (above, Send(kappa, first, kw, end, k_send.at[2], k_recv.at[2], (tm, s - 1))),
        (above, Send(rate, first, rw, end, k_send.at[3], k_recv.at[3], (tm, s - 1))),
        (even & below, Send(own, last, gb, upper, g_send.at[0], g_recv.at[0], (tm, s + 1))),
        (even & above, Send(own, first, gb, lower, g_send.at[1], g_recv.at[0], (tm + 1, s - 1))),
        (odd & later & below, Send(own, last, ga, upper, g_send.at[0], g_recv.at[2], (tm + 1, s + 1))),
        (odd & later & above, Send(own, first, ga, lower, g_send.at[1], g_recv.at[2], (tm + 2, s - 1))),
        (even, Send(own, tail, gb, main_odd, g_send.at[2], g_recv.at[1], (partner, s))),
        (odd & later, Send(own, tail, ga, main_odd, g_send.at[2], g_recv.at[3], (tm + 2, s))),
    ]
    piece = main // PIECES
    relays = [
        Send(own, (i * piece, piece), st, pl.ds(i * piece, piece), t_send.at[i], t_recv.at[i], (partner, s))
        for i in range(PIECES)
    ]
    onward = [
        copy(st.at[:, pl.ds(i * piece, piece)], ga.at[:, pl.ds(PAD + halo + i * piece, piece)],
             o_send.at[i], o_recv.at[i], (tm + 2, s))
        for i in range(PIECES)
    ]
    halves, fields = sends[:4], sends[4:]
    count = sum(condition.astype(jnp.int32) for condition, _ in targets)
    pl.semaphore_wait(barrier, count)
    for condition, transfer in sends:
        @pl.when(condition)
        def _(transfer=transfer):
            transfer.start()

    @pl.when(odd & later)
    def _():
        for relay in relays:
            relay.start()

    zeros = jnp.zeros((tiles, PAD, LANES), jnp.float32)
    for ref in (ga, gb, x_ref, ya, yb, z_ref, w_ref, cr, vo, vw, u1, u2):
        ref[:, pl.ds(0, PAD), :] = zeros
        ref[:, pl.ds(ref.shape[1] - PAD, PAD), :] = zeros
    rim = jnp.zeros((tiles, 2 * STEPS, LANES), jnp.float32)
    for ref in (cr, vo):
        ref[:, pl.ds(PAD, 2 * STEPS), :] = rim
        ref[:, pl.ds(wide - PAD - 2 * STEPS, 2 * STEPS), :] = rim
    blank = jnp.zeros((tiles, halo, LANES), jnp.float32)

    @pl.when(even & ~above)
    def _():
        ga[:, upper, :] = blank
        gb[:, upper, :] = blank

    @pl.when(odd & ~below)
    def _():
        ga[:, lower, :] = blank
        gb[:, lower, :] = blank

    @pl.when(~above)
    def _():
        kw[:, upper, :] = blank
        rw[:, upper, :] = blank

    @pl.when(~below)
    def _():
        kw[:, end, :] = blank
        rw[:, end, :] = blank

    @pl.when(even & later)
    def _():
        for relay, step_on in zip(relays, onward):
            relay.wait_recv()
            step_on.start()

    k_local[1]()
    r_local[1]()

    @pl.when(above)
    def _():
        halves[0][1].wait_recv()
        halves[1][1].wait_recv()

    @pl.when(below)
    def _():
        halves[2][1].wait_recv()
        halves[3][1].wait_recv()

    def scaled(index, carry):
        part = pl.ds(pl.multiple_of(index * 32 + PAD, 8), 32)
        k = DIFFUSION * kw[:, part, :]
        kw[:, part, :] = k
        aw[:, part, :] = (1.0 + rw[:, part, :]) - 4.0 * k
        return carry

    lax.fori_loop(0, (rows + 2 * halo) // 32, scaled, 0)

    def step(src, low, size, offset, emit):
        lane = lax.broadcasted_iota(jnp.int32, (size, LANES), 1)
        at = pl.ds(pl.multiple_of(low + offset, 8), size)
        here = pl.ds(pl.multiple_of(low, 8), size)
        centre = src[0, here, :]
        before = after = 0.0
        to_left = pltpu.roll(centre, LANES - 1, 1)
        for t in range(tiles):
            to_right = pltpu.roll(centre, 1, 1)
            if t + 1 < tiles:
                following = src[t + 1, here, :]
                after = pltpu.roll(following, LANES - 1, 1)
            else:
                following, after = None, 0.0
            left = jnp.where(lane == 0, before, to_right)
            right = jnp.where(lane == LANES - 1, after, to_left)
            beside = src[t, pl.ds(low - 1, size), :] + src[t, pl.ds(low + 1, size), :]
            total = beside + (left + right)
            own_part = centre * (aw[t, at, :] - rw[t, at, :] * (centre * centre))
            emit(t, own_part + kw[t, at, :] * total, centre)
            before, centre, to_left = to_right, following, after

    def over(start, stop, act):
        size = block_of(stop - start)
        count = (stop - start) // size

        def body(index, carry):
            act(index * size + start, size)
            return carry

        lax.fori_loop(0, count, body, 0, unroll=True)

    def sweep(src, dst, start=PAD, stop=wide - PAD, offset=shift):
        def act(low, size):
            def emit(t, value, centre):
                dst[t, pl.ds(pl.multiple_of(low, 8), size), :] = value

            step(src, low, size, offset, emit)

        over(start, stop, act)

    def march(src, scratch, dst, times):
        for turn in range(times):
            out = dst if (times - 1 - turn) % 2 == 0 else scratch
            sweep(src, out)
            src = out

    def defects(field, relaxed, out, weight):
        march(field, x_ref, relaxed, STEPS)
        sweep(relaxed, w_ref)
        march(w_ref, z_ref, x_ref, STEPS - 2)

        def act(low, size):
            here = pl.ds(pl.multiple_of(low, 8), size)

            def emit(t, fine, centre):
                coarse = coarse_scale * w_ref[t, here, :] - (coarse_scale - 1.0) * relaxed[t, here, :]
                out[t, here, :] = fine - weight * coarse

            step(x_ref, low, size, shift, emit)

        over(PAD, wide - PAD, act)

    @pl.when(later)
    def _():
        @pl.when(even)
        def _():
            g_local[1]()

        @pl.when(even & above)
        def _():
            fields[0][1].wait_recv()

        @pl.when(odd & below)
        def _():
            fields[1][1].wait_recv()

        @pl.when(odd)
        def _():
            fields[4][1].wait_recv()

        defects(gb, yb, db, jnp.where(p == 0, 0.0, 1.0))

    @pl.when(earlier)
    def _():
        @pl.when(even & above)
        def _():
            fields[2][1].wait_recv()

        @pl.when(odd & below)
        def _():
            fields[3][1].wait_recv()

        @pl.when(even)
        def _():
            for step_on in onward:
                step_on.wait_recv()

        @pl.when(odd)
        def _():
            fields[5][1].wait_recv()

        defects(ga, ya, da, 1.0)

    base = PAD + 2 * STEPS

    def chunk(index):
        return pl.ds(pl.multiple_of(index * CHUNK + base, 8), CHUNK)

    def chain(index):
        part = chunk(index)
        return copy(ve.at[:, part], cr.at[:, part], c_send.at[index], c_recv.at[index], (tm + 2, s))

    def target(index, side):
        return pl.ds(pl.multiple_of(index * CHUNK + PAD + side * half, 8), CHUNK)

    def forward(index, src):
        return copy(
            src.at[:, chunk(index)], vw.at[:, target(index, b)], f_send.at[index], f_recv.at[index],
            (partner, s),
        )

    def hand_over(index):
        @pl.when(even & (index < kept))
        def _():
            forward(index, vo).start()
            vw[:, target(index, 0), :] = cr[:, chunk(index), :]

        @pl.when(odd & (index >= skipped))
        def _():
            forward(index, cr).start()
            vw[:, target(index, 1), :] = vo[:, chunk(index), :]

    def corrected(src, defect, out, index):
        here = chunk(index)

        def emit(t, value, centre):
            image = coarse_scale * value - (coarse_scale - 1.0) * centre
            out[t, here, :] = image + defect[t, here, :]

        step(src, index * CHUNK + base, CHUNK, shift, emit)

    @pl.when(p == 0)
    def _():
        def body(index, carry):
            part = chunk(index)
            ve[:, part, :] = db[:, part, :]
            chain(index).start()
            vo[:, part, :] = yb[:, part, :]
            cr[:, part, :] = gb[:, part, :]
            hand_over(index)
            return carry

        lax.fori_loop(0, chunks, body, 0)

    @pl.when(earlier)
    def _():
        def body(index, carry):
            @pl.when(index < chunks)
            def _():
                chain(index).wait_recv()

            @pl.when((index >= 1) & (index <= chunks))
            def _():
                corrected(cr, da, vo, index - 1)

            @pl.when((index >= 2) & later)
            def _():
                corrected(vo, db, ve, index - 2)
                chain(index - 2).start()

            @pl.when((index >= 1) & (index <= chunks))
            def _():
                hand_over(index - 1)

            return carry

        lax.fori_loop(0, chunks + 2, body, 0)

    def collect(index, carry):
        forward(index + skipped * (1 - b), vo).wait_recv()
        return carry

    lax.fori_loop(0, kept, collect, 0)

    offset = halo - margin
    src = vw
    for turn in range(STEPS - 2):
        out = u1 if turn % 2 == 0 else u2
        sweep(src, out, PAD, full - PAD, offset)
        src = out

    def finish(low, size):
        out = pl.ds(pl.multiple_of(low - PAD - margin, 8), size)

        def emit(t, value, centre):
            lanes = pl.ds(t * LANES, LANES)
            f_out[0, out, lanes] = value
            c_out[0, out, lanes] = vw[t, pl.ds(pl.multiple_of(low, 8), size), :]

        step(src, low, size, offset, emit)

    over(PAD + margin, PAD + margin + rows, finish)

    @pl.when(~later & even)
    def _():
        g_local[1]()

    @pl.when(~later)
    def _():
        @pl.when(even & above)
        def _():
            fields[0][1].wait_recv()

        @pl.when(odd & below)
        def _():
            fields[1][1].wait_recv()

        @pl.when(odd)
        def _():
            fields[4][1].wait_recv()

    for condition, transfer in sends:
        @pl.when(condition)
        def _(transfer=transfer):
            transfer.wait_send()

    @pl.when(later)
    def _():
        def body(index, carry):
            chain(index).wait_send()
            return carry

        lax.fori_loop(0, chunks, body, 0)

    @pl.when(odd & later)
    def _():
        for relay in relays:
            relay.wait_send()

    @pl.when(even & later)
    def _():
        for step_on in onward:
            step_on.wait_send()

    def sent(index, carry):
        forward(index + skipped * b, vo).wait_send()
        return carry

    lax.fori_loop(0, kept, sent, 0)


def halo_of(points):
    needed = 2 * STEPS + max(points - 3, 0) + STEPS - 1
    return -(-needed // CHUNK) * CHUNK


def chained(points, strips, guess, kappa, rate):
    rows, width = kappa.shape
    tiles = width // LANES
    halo = halo_of(points)
    margin = halo - 2 * STEPS
    wide = rows // 2 + 2 * halo + 2 * PAD
    full = rows + 2 * margin + 2 * PAD
    chunks = (rows // 2 + 2 * margin) // CHUNK
    f32 = jnp.float32

    def held(height):
        return pltpu.VMEM((tiles, height, LANES), f32)

    part, whole, coefficient = held(wide), held(full), held(rows + 2 * halo + 2 * PAD)
    dma = pltpu.SemaphoreType.DMA
    vmem = pl.BlockSpec(memory_space=pltpu.VMEM)
    anywhere = pl.BlockSpec(memory_space=pltpu.HBM)
    return pl.pallas_call(
        functools.partial(kernel, points, strips),
        out_shape=[jax.ShapeDtypeStruct(guess.shape, f32)] * 2,
        in_specs=[anywhere] * 3,
        out_specs=[vmem] * 2,
        scratch_shapes=[coefficient] * 3 + [part] * 12 + [whole] * 3 + [held(rows // 2 + halo)]
        + [dma((3,))] + [dma((4,))] * 4 + [dma((chunks,))] * 4 + [dma((PIECES,))] * 4,
        compiler_params=pltpu.CompilerParams(
            collective_id=0, has_side_effects=True, vmem_limit_bytes=63 * 2**20
        ),
    )(guess, kappa, rate)


def extended(shard, sides, width):
    for axis, dim in sides:
        peers, length = (lax.axis_size(axis), shard.shape[dim])
        up = [(i, (i + 1) % peers) for i in range(peers - 1)]
        down = [(j, i) for i, j in up]
        last = lax.slice_in_dim(shard, length - width, length, axis=dim)
        initial = lax.slice_in_dim(shard, 0, width, axis=dim)
        before = lax.ppermute(last, axis, up)
        after = lax.ppermute(initial, axis, down)
        shard = jnp.concatenate([before, shard, after], axis=dim)
    return shard


def from_behind(value, axis, steps):
    count = lax.axis_size(axis)
    initial, last = (max(0, -steps), min(count, count - steps))
    return lax.ppermute(value, axis, [(source, source + steps) for source in range(initial, last)])


def advance_padded(padded, kappa, rate, scale):
    centre = padded[1:-1, 1:-1]
    laplace = (
        padded[2:, 1:-1] + padded[:-2, 1:-1] + padded[1:-1, 2:] + padded[1:-1, :-2] - 4.0 * centre
    )
    return centre + scale * (
        DIFFUSION * kappa * laplace + rate * (centre - centre * centre * centre)
    )


def deep_border(state, count):
    return extended(state, (("space", 0),), count)


def deep_step(wide, margin, widened, scale):
    rows = widened.shape[1] - 2 * STEPS
    height = wide.shape[0] - 2
    lower = STEPS - (margin - 1)
    kappa_rows = widened[0, lower : lower + height]
    rate_rows = widened[1, lower : lower + height]
    stepped = advance_padded(jnp.pad(wide, ((0, 0), (1, 1))), kappa_rows, rate_rows, scale)
    strip = lax.axis_index("space")
    total = rows * lax.axis_size("space")
    global_rows = strip * rows - (margin - 1) + lax.broadcasted_iota(jnp.int32, stepped.shape, 0)
    inside = (global_rows >= 0) & (global_rows < total)
    return jnp.where(inside, stepped, jnp.zeros_like(stepped))


def deep_march(wide, margin, widened, count):
    for repeat in range(count):
        wide = deep_step(wide, margin, widened, 1.0)
        margin = margin - 1
    return wide


def forward(state):
    return from_behind(state, "tm", 1)


def local(guess, kappa, rate):
    position = lax.axis_index("tm")
    member = position % GROUP
    coarse_scale = float(STEPS)
    state = guess[0]
    incoming = forward(state)
    widened = extended(jnp.stack([kappa, rate]), (("space", 1),), STEPS)
    marched = deep_march(deep_border(incoming, STEPS), STEPS, widened, STEPS)
    relaxed = jnp.where(position == 0, state, marched)
    incoming = forward(relaxed)
    wide = deep_border(incoming, STEPS)
    rows = relaxed.shape[0]
    band = jnp.pad(wide[STEPS - 1 : STEPS + rows + 1], ((0, 0), (1, 1)))
    coarse_image = advance_padded(band, kappa, rate, coarse_scale)
    fine_image = deep_march(wide, STEPS, widened, STEPS)
    defect = jnp.where(position == 0, jnp.zeros_like(fine_image), fine_image - coarse_image)
    coarse = relaxed
    for sweep_number in range(SWEEPS):
        for turn in range(GROUP):
            arrived = from_behind(coarse, "tm", 1)
            framed = extended(arrived, (("space", 0),), 1)
            framed = jnp.pad(framed, ((0, 0), (1, 1)))
            updated = advance_padded(framed, kappa, rate, coarse_scale) + defect
            if turn + 1 < GROUP:
                active = member == turn + 1
            else:
                active = (member == 0) & (position >= GROUP)
            coarse = jnp.where(active, updated, coarse)
    last_fine = deep_march(deep_border(coarse, STEPS - 1), STEPS - 1, widened, STEPS - 1)
    return (coarse[None], last_fine[None])


def solution(mesh):
    points, strips = mesh.shape["tm"], mesh.shape["space"]

    def run(guess, kappa, rate):
        rows, width = kappa.shape
        settled = points <= GROUP * SWEEPS and points % 2 == 0 and points >= 4
        aligned = rows % 32 == 0 and width % LANES == 0 and (2 * STEPS) % 8 == 0
        if settled and aligned and halo_of(points) % 16 == 0 and (rows // 2 + halo_of(points)) % (8 * PIECES) == 0 and 2 * halo_of(points) <= rows:
            return tuple(chained(points, strips, guess, kappa, rate))
        return local(guess, kappa, rate)

    return jax.shard_map(
        run,
        mesh=mesh,
        in_specs=(P("tm", "space", None), P("space", None), P("space", None)),
        out_specs=(P("tm", "space", None), P("tm", "space", None)),
        check_vma=False,
    )
```

```python
import functools
import jax
import jax.numpy as jnp
from jax import lax
from jax.experimental import pallas as pl
from jax.experimental.pallas import tpu as pltpu
from jax.sharding import PartitionSpec as P

STEPS = 4
GROUP = 4
SWEEPS = 2


DIFFUSION = 0.05
PAD = 8
CHUNK = 8
PIECES = 9
LANES = 128
MESH = pl.DeviceIdType.MESH


def block_of(rows):
    return max(size for size in range(8, min(rows, 32) + 1, 8) if rows % size == 0)


def kernel(
    points, strips, guess, kappa, rate, c_out, f_out,
    kw, rw, aw, ga, gb, x_ref, ya, yb, z_ref, w_ref, da, db, cr, vo, ve, vw, u1, u2, st,
    local_sem, k_send, k_recv, g_send, g_recv, c_send, c_recv, f_send, f_recv,
    t_send, t_recv, o_send, o_recv,
):
    rows, width = kappa.shape
    tiles = width // LANES
    half = rows // 2
    wide = ga.shape[1]
    full = vw.shape[1]
    halo = (wide - 2 * PAD - half) // 2
    margin = halo - 2 * STEPS
    chunks = (half + 2 * margin) // CHUNK
    skipped = margin // CHUNK
    kept = chunks - skipped
    pairs = points // 2
    tm, s = lax.axis_index("tm"), lax.axis_index("space")
    p, b = tm // 2, tm % 2
    coarse_scale = float(STEPS)
    shift = b * half
    partner = p * 2 + (1 - b)

    later, earlier = p < pairs - 1, p > 0
    below, above = s < strips - 1, s > 0
    even, odd = b == 0, b == 1

    targets = [
        (below, (tm, s + 1)), (above, (tm, s - 1)), (s >= 0, (partner, s)),
        (even & above, (tm + 1, s - 1)), (later, (tm + 2, s)),
        (odd & later & below, (tm + 1, s + 1)),
        (odd & later & above, (tm + 2, s - 1)),
    ]
    sources = [
        (below, (tm, s + 1)), (above, (tm, s - 1)), (s >= 0, (partner, s)),
        (odd & below, (tm - 1, s + 1)), (earlier, (tm - 2, s)),
        (even & earlier & above, (tm - 1, s - 1)),
        (odd & earlier & below, (tm - 2, s + 1)),
    ]
    barrier = pltpu.get_barrier_semaphore()
    for condition, device in sources:
        @pl.when(condition)
        def _(device=device):
            pl.semaphore_signal(barrier, inc=1, device_id=device, device_id_type=MESH)

    main = half + halo
    cut = PAD + (wide - 2 * PAD) // 16 * 8
    early = cut + 8 - PAD
    early_odd, late_odd = pl.ds(PAD, early), pl.ds(PAD + early, main - early)
    first, last = (0, halo), (rows - halo, halo)
    head = (0, main)
    tails = (rows - main, early), (rows - main + early, main - early)
    upper, lower = pl.ds(PAD, halo), pl.ds(PAD + main, halo)
    main_even = pl.ds(PAD + halo, main)
    end = pl.ds(PAD + halo + rows, halo)
    middle = pl.ds(PAD + halo, rows)
    own = guess.at[0]

    def columns(src, part):
        start, count = part
        return [src.at[pl.ds(start, count), pl.ds(t * LANES, LANES)] for t in range(tiles)]

    def fetch(src, part, dst, place, sem):
        def start():
            for t, column in enumerate(columns(src, part)):
                pltpu.make_async_copy(column, dst.at[t, place], sem).start()

        def wait():
            pltpu.make_async_copy(dst.at[:, place], dst.at[:, place], sem).wait()

        return start, wait

    def copy(src, dst, send, recv, device):
        return pltpu.make_async_remote_copy(
            src_ref=src, dst_ref=dst, send_sem=send, recv_sem=recv,
            device_id=device, device_id_type=MESH,
        )

    class Send:
        def __init__(self, src, part, dst, place, send, recv, device):
            self.start_all = [
                copy(column, dst.at[t, place], send, recv, device)
                for t, column in enumerate(columns(src, part))
            ]
            self.whole = copy(dst.at[:, place], dst.at[:, place], send, recv, device)

        def start(self):
            for one in self.start_all:
                one.start()

        def wait_recv(self):
            self.whole.wait_recv()

        def wait_send(self):
            self.whole.wait_send()

    k_local = fetch(kappa, (0, rows), kw, middle, local_sem.at[0])
    r_local = fetch(rate, (0, rows), rw, middle, local_sem.at[1])
    g_local = fetch(own, head, gb, main_even, local_sem.at[2])
    k_local[0]()
    r_local[0]()

    @pl.when(even)
    def _():
        g_local[0]()

    sends = [
        (below, Send(kappa, last, kw, upper, k_send.at[0], k_recv.at[0], (tm, s + 1))),
        (below, Send(rate, last, rw, upper, k_send.at[1], k_recv.at[1], (tm, s + 1))),
        (above, Send(kappa, first, kw, end, k_send.at[2], k_recv.at[2], (tm, s - 1))),
        (above, Send(rate, first, rw, end, k_send.at[3], k_recv.at[3], (tm, s - 1))),
        (even & below, Send(own, last, gb, upper, g_send.at[0], g_recv.at[0], (tm, s + 1))),
        (even & above, Send(own, first, gb, lower, g_send.at[1], g_recv.at[0], (tm + 1, s - 1))),
        (odd & later & below, Send(own, last, ga, upper, g_send.at[0], g_recv.at[2], (tm + 1, s + 1))),
        (odd & later & above, Send(own, first, ga, lower, g_send.at[1], g_recv.at[2], (tm + 2, s - 1))),
        (even, Send(own, tails[0], gb, early_odd, g_send.at[2], g_recv.at[1], (partner, s))),
        (odd & later, Send(own, tails[0], ga, early_odd, g_send.at[2], g_recv.at[3], (tm + 2, s))),
        (even, Send(own, tails[1], gb, late_odd, g_send.at[3], g_recv.at[4], (partner, s))),
        (odd & later, Send(own, tails[1], ga, late_odd, g_send.at[3], g_recv.at[5], (tm + 2, s))),
    ]
    piece = main // PIECES
    relays = [
        Send(own, (i * piece, piece), st, pl.ds(i * piece, piece), t_send.at[i], t_recv.at[i], (partner, s))
        for i in range(PIECES)
    ]
    onward = [
        copy(st.at[:, pl.ds(i * piece, piece)], ga.at[:, pl.ds(PAD + halo + i * piece, piece)],
             o_send.at[i], o_recv.at[i], (tm + 2, s))
        for i in range(PIECES)
    ]
    halves, fields = sends[:4], sends[4:]
    count = sum(condition.astype(jnp.int32) for condition, _ in targets)
    pl.semaphore_wait(barrier, count)
    for condition, transfer in sends:
        @pl.when(condition)
        def _(transfer=transfer):
            transfer.start()

    @pl.when(odd & later)
    def _():
        for relay in relays:
            relay.start()

    zeros = jnp.zeros((tiles, PAD, LANES), jnp.float32)
    for ref in (ga, gb, x_ref, ya, yb, z_ref, w_ref, cr, vo, vw, u1, u2):
        ref[:, pl.ds(0, PAD), :] = zeros
        ref[:, pl.ds(ref.shape[1] - PAD, PAD), :] = zeros
    rim = jnp.zeros((tiles, 2 * STEPS, LANES), jnp.float32)
    for ref in (cr, vo):
        ref[:, pl.ds(PAD, 2 * STEPS), :] = rim
        ref[:, pl.ds(wide - PAD - 2 * STEPS, 2 * STEPS), :] = rim
    blank = jnp.zeros((tiles, halo, LANES), jnp.float32)

    @pl.when(even & ~above)
    def _():
        ga[:, upper, :] = blank
        gb[:, upper, :] = blank

    @pl.when(odd & ~below)
    def _():
        ga[:, lower, :] = blank
        gb[:, lower, :] = blank

    @pl.when(~above)
    def _():
        kw[:, upper, :] = blank
        rw[:, upper, :] = blank

    @pl.when(~below)
    def _():
        kw[:, end, :] = blank
        rw[:, end, :] = blank

    k_local[1]()
    r_local[1]()

    @pl.when(above)
    def _():
        halves[0][1].wait_recv()
        halves[1][1].wait_recv()

    @pl.when(below)
    def _():
        halves[2][1].wait_recv()
        halves[3][1].wait_recv()

    def scaled(index, carry):
        part = pl.ds(pl.multiple_of(index * 32 + PAD, 8), 32)
        k = DIFFUSION * kw[:, part, :]
        kw[:, part, :] = k
        aw[:, part, :] = (1.0 + rw[:, part, :]) - 4.0 * k
        return carry

    lax.fori_loop(0, (rows + 2 * halo) // 32, scaled, 0)

    def step(src, low, size, offset, emit):
        lane = lax.broadcasted_iota(jnp.int32, (size, LANES), 1)
        at = pl.ds(pl.multiple_of(low + offset, 8), size)
        here = pl.ds(pl.multiple_of(low, 8), size)
        centre = src[0, here, :]
        before = after = 0.0
        to_left = pltpu.roll(centre, LANES - 1, 1)
        for t in range(tiles):
            to_right = pltpu.roll(centre, 1, 1)
            if t + 1 < tiles:
                following = src[t + 1, here, :]
                after = pltpu.roll(following, LANES - 1, 1)
            else:
                following, after = None, 0.0
            left = jnp.where(lane == 0, before, to_right)
            right = jnp.where(lane == LANES - 1, after, to_left)
            beside = src[t, pl.ds(low - 1, size), :] + src[t, pl.ds(low + 1, size), :]
            total = beside + (left + right)
            own_part = centre * (aw[t, at, :] - rw[t, at, :] * (centre * centre))
            emit(t, own_part + kw[t, at, :] * total, centre)
            before, centre, to_left = to_right, following, after

    def over(start, stop, act):
        size = block_of(stop - start)
        count = (stop - start) // size

        def body(index, carry):
            act(index * size + start, size)
            return carry

        lax.fori_loop(0, count, body, 0, unroll=True)

    def sweep(src, dst, start=PAD, stop=wide - PAD, offset=shift):
        def act(low, size):
            def emit(t, value, centre):
                dst[t, pl.ds(pl.multiple_of(low, 8), size), :] = value

            step(src, low, size, offset, emit)

        over(start, stop, act)

    def march(src, pair, dst, times, start, stop, keep):
        for turn in range(times):
            out = dst if turn == times - 1 else pair[turn % 2]
            sweep(src, out, keep if turn == times - 1 else start, stop)
            src = out

    def defects(field, relaxed, out, weight, start, stop, keep):
        march(field, (x_ref, z_ref), relaxed, STEPS, start, stop, keep)
        sweep(relaxed, w_ref, start, stop)
        march(w_ref, (z_ref, x_ref), x_ref, STEPS - 2, start, stop, start)

        def act(low, size):
            here = pl.ds(pl.multiple_of(low, 8), size)

            def emit(t, fine, centre):
                coarse = coarse_scale * w_ref[t, here, :] - (coarse_scale - 1.0) * relaxed[t, here, :]
                out[t, here, :] = fine - weight * coarse

            step(x_ref, low, size, shift, emit)

        over(keep, stop, act)

    early_rows = (PAD, cut, PAD)
    late_rows = (cut - 4 * STEPS, wide - PAD, cut - 2 * STEPS)
    needed = -(-(cut + 1 - PAD - halo) // piece)
    weight = jnp.where(p == 0, 0.0, 1.0)

    def relay_on(start, stop):
        @pl.when(even & later)
        def _():
            for i in range(start, stop):
                relays[i].wait_recv()
                onward[i].start()

    @pl.when(even)
    def _():
        g_local[1]()

    @pl.when(even & above)
    def _():
        fields[0][1].wait_recv()

    @pl.when(odd & below)
    def _():
        fields[1][1].wait_recv()

    @pl.when(odd)
    def _():
        fields[4][1].wait_recv()

    @pl.when(later)
    def _():
        defects(gb, yb, db, weight, *early_rows)

    relay_on(0, needed - 1)

    @pl.when(even & later)
    def _():
        defects(gb, yb, db, weight, *late_rows)

    relay_on(needed - 1, PIECES - 2)

    @pl.when(earlier)
    def _():
        @pl.when(even & above)
        def _():
            fields[2][1].wait_recv()

        @pl.when(odd & below)
        def _():
            fields[3][1].wait_recv()

        @pl.when(even)
        def _():
            for step_on in onward[:needed]:
                step_on.wait_recv()

        @pl.when(odd)
        def _():
            fields[5][1].wait_recv()

        defects(ga, ya, da, 1.0, *early_rows)

    relay_on(PIECES - 2, PIECES)

    @pl.when(odd)
    def _():
        fields[6][1].wait_recv()

    @pl.when(odd & later)
    def _():
        defects(gb, yb, db, weight, *late_rows)

    @pl.when(earlier)
    def _():
        @pl.when(even)
        def _():
            for step_on in onward[needed:]:
                step_on.wait_recv()

        @pl.when(odd)
        def _():
            fields[7][1].wait_recv()

        defects(ga, ya, da, 1.0, *late_rows)

    base = PAD + 2 * STEPS

    def chunk(index):
        return pl.ds(pl.multiple_of(index * CHUNK + base, 8), CHUNK)

    def chain(index):
        part = chunk(index)
        return copy(ve.at[:, part], cr.at[:, part], c_send.at[index], c_recv.at[index], (tm + 2, s))

    def target(index, side):
        return pl.ds(pl.multiple_of(index * CHUNK + PAD + side * half, 8), CHUNK)

    def forward(index, src):
        return copy(
            src.at[:, chunk(index)], vw.at[:, target(index, b)], f_send.at[index], f_recv.at[index],
            (partner, s),
        )

    def hand_over(index):
        @pl.when(even & (index < kept))
        def _():
            forward(index, vo).start()
            vw[:, target(index, 0), :] = cr[:, chunk(index), :]

        @pl.when(odd & (index >= skipped))
        def _():
            forward(index, cr).start()
            vw[:, target(index, 1), :] = vo[:, chunk(index), :]

    def corrected(src, defect, out, index):
        here = chunk(index)

        def emit(t, value, centre):
            image = coarse_scale * value - (coarse_scale - 1.0) * centre
            out[t, here, :] = image + defect[t, here, :]

        step(src, index * CHUNK + base, CHUNK, shift, emit)

    @pl.when(p == 0)
    def _():
        def body(index, carry):
            part = chunk(index)
            ve[:, part, :] = db[:, part, :]
            chain(index).start()
            vo[:, part, :] = yb[:, part, :]
            cr[:, part, :] = gb[:, part, :]
            hand_over(index)
            return carry

        lax.fori_loop(0, chunks, body, 0)

    @pl.when(earlier)
    def _():
        def body(index, carry):
            @pl.when(index < chunks)
            def _():
                chain(index).wait_recv()

            @pl.when((index >= 1) & (index <= chunks))
            def _():
                corrected(cr, da, vo, index - 1)

            @pl.when((index >= 2) & later)
            def _():
                corrected(vo, db, ve, index - 2)
                chain(index - 2).start()

            @pl.when((index >= 1) & (index <= chunks))
            def _():
                hand_over(index - 1)

            return carry

        lax.fori_loop(0, chunks + 2, body, 0)

    def collect(index, carry):
        forward(index + skipped * (1 - b), vo).wait_recv()
        return carry

    lax.fori_loop(0, kept, collect, 0)

    offset = halo - margin
    src = vw
    for turn in range(STEPS - 2):
        out = u1 if turn % 2 == 0 else u2
        sweep(src, out, PAD, full - PAD, offset)
        src = out

    def finish(low, size):
        out = pl.ds(pl.multiple_of(low - PAD - margin, 8), size)

        def emit(t, value, centre):
            lanes = pl.ds(t * LANES, LANES)
            f_out[0, out, lanes] = value
            c_out[0, out, lanes] = vw[t, pl.ds(pl.multiple_of(low, 8), size), :]

        step(src, low, size, offset, emit)

    over(PAD + margin, PAD + margin + rows, finish)

    for condition, transfer in sends:
        @pl.when(condition)
        def _(transfer=transfer):
            transfer.wait_send()

    @pl.when(later)
    def _():
        def body(index, carry):
            chain(index).wait_send()
            return carry

        lax.fori_loop(0, chunks, body, 0)

    @pl.when(odd & later)
    def _():
        for relay in relays:
            relay.wait_send()

    @pl.when(even & later)
    def _():
        for step_on in onward:
            step_on.wait_send()

    def sent(index, carry):
        forward(index + skipped * b, vo).wait_send()
        return carry

    lax.fori_loop(0, kept, sent, 0)


def halo_of(points):
    needed = 2 * STEPS + max(points - 3, 0) + STEPS - 1
    return -(-needed // CHUNK) * CHUNK


def chained(points, strips, guess, kappa, rate):
    rows, width = kappa.shape
    tiles = width // LANES
    halo = halo_of(points)
    margin = halo - 2 * STEPS
    wide = rows // 2 + 2 * halo + 2 * PAD
    full = rows + 2 * margin + 2 * PAD
    chunks = (rows // 2 + 2 * margin) // CHUNK
    f32 = jnp.float32

    def held(height):
        return pltpu.VMEM((tiles, height, LANES), f32)

    part, whole, coefficient = held(wide), held(full), held(rows + 2 * halo + 2 * PAD)
    dma = pltpu.SemaphoreType.DMA
    vmem = pl.BlockSpec(memory_space=pltpu.VMEM)
    anywhere = pl.BlockSpec(memory_space=pltpu.HBM)
    return pl.pallas_call(
        functools.partial(kernel, points, strips),
        out_shape=[jax.ShapeDtypeStruct(guess.shape, f32)] * 2,
        in_specs=[anywhere] * 3,
        out_specs=[vmem] * 2,
        scratch_shapes=[coefficient] * 3 + [part] * 12 + [whole] * 3 + [held(rows // 2 + halo)]
        + [dma((3,))] + [dma((4,))] * 3 + [dma((6,))] + [dma((chunks,))] * 4 + [dma((PIECES,))] * 4,
        compiler_params=pltpu.CompilerParams(
            collective_id=0, has_side_effects=True, vmem_limit_bytes=63 * 2**20
        ),
    )(guess, kappa, rate)


def extended(shard, sides, width):
    for axis, dim in sides:
        peers, length = (lax.axis_size(axis), shard.shape[dim])
        up = [(i, (i + 1) % peers) for i in range(peers - 1)]
        down = [(j, i) for i, j in up]
        last = lax.slice_in_dim(shard, length - width, length, axis=dim)
        initial = lax.slice_in_dim(shard, 0, width, axis=dim)
        before = lax.ppermute(last, axis, up)
        after = lax.ppermute(initial, axis, down)
        shard = jnp.concatenate([before, shard, after], axis=dim)
    return shard


def from_behind(value, axis, steps):
    count = lax.axis_size(axis)
    initial, last = (max(0, -steps), min(count, count - steps))
    return lax.ppermute(value, axis, [(source, source + steps) for source in range(initial, last)])


def advance_padded(padded, kappa, rate, scale):
    centre = padded[1:-1, 1:-1]
    laplace = (
        padded[2:, 1:-1] + padded[:-2, 1:-1] + padded[1:-1, 2:] + padded[1:-1, :-2] - 4.0 * centre
    )
    return centre + scale * (
        DIFFUSION * kappa * laplace + rate * (centre - centre * centre * centre)
    )


def deep_border(state, count):
    return extended(state, (("space", 0),), count)


def deep_step(wide, margin, widened, scale):
    rows = widened.shape[1] - 2 * STEPS
    height = wide.shape[0] - 2
    lower = STEPS - (margin - 1)
    kappa_rows = widened[0, lower : lower + height]
    rate_rows = widened[1, lower : lower + height]
    stepped = advance_padded(jnp.pad(wide, ((0, 0), (1, 1))), kappa_rows, rate_rows, scale)
    strip = lax.axis_index("space")
    total = rows * lax.axis_size("space")
    global_rows = strip * rows - (margin - 1) + lax.broadcasted_iota(jnp.int32, stepped.shape, 0)
    inside = (global_rows >= 0) & (global_rows < total)
    return jnp.where(inside, stepped, jnp.zeros_like(stepped))


def deep_march(wide, margin, widened, count):
    for repeat in range(count):
        wide = deep_step(wide, margin, widened, 1.0)
        margin = margin - 1
    return wide


def forward(state):
    return from_behind(state, "tm", 1)


def local(guess, kappa, rate):
    position = lax.axis_index("tm")
    member = position % GROUP
    coarse_scale = float(STEPS)
    state = guess[0]
    incoming = forward(state)
    widened = extended(jnp.stack([kappa, rate]), (("space", 1),), STEPS)
    marched = deep_march(deep_border(incoming, STEPS), STEPS, widened, STEPS)
    relaxed = jnp.where(position == 0, state, marched)
    incoming = forward(relaxed)
    wide = deep_border(incoming, STEPS)
    rows = relaxed.shape[0]
    band = jnp.pad(wide[STEPS - 1 : STEPS + rows + 1], ((0, 0), (1, 1)))
    coarse_image = advance_padded(band, kappa, rate, coarse_scale)
    fine_image = deep_march(wide, STEPS, widened, STEPS)
    defect = jnp.where(position == 0, jnp.zeros_like(fine_image), fine_image - coarse_image)
    coarse = relaxed
    for sweep_number in range(SWEEPS):
        for turn in range(GROUP):
            arrived = from_behind(coarse, "tm", 1)
            framed = extended(arrived, (("space", 0),), 1)
            framed = jnp.pad(framed, ((0, 0), (1, 1)))
            updated = advance_padded(framed, kappa, rate, coarse_scale) + defect
            if turn + 1 < GROUP:
                active = member == turn + 1
            else:
                active = (member == 0) & (position >= GROUP)
            coarse = jnp.where(active, updated, coarse)
    last_fine = deep_march(deep_border(coarse, STEPS - 1), STEPS - 1, widened, STEPS - 1)
    return (coarse[None], last_fine[None])


def solution(mesh):
    points, strips = mesh.shape["tm"], mesh.shape["space"]

    def run(guess, kappa, rate):
        rows, width = kappa.shape
        settled = points <= GROUP * SWEEPS and points % 2 == 0 and points >= 4
        aligned = rows % 32 == 0 and width % LANES == 0 and (2 * STEPS) % 8 == 0
        if settled and aligned and halo_of(points) % 16 == 0 and (rows // 2 + halo_of(points)) % (8 * PIECES) == 0 and 2 * halo_of(points) <= rows:
            return tuple(chained(points, strips, guess, kappa, rate))
        return local(guess, kappa, rate)

    return jax.shard_map(
        run,
        mesh=mesh,
        in_specs=(P("tm", "space", None), P("space", None), P("space", None)),
        out_specs=(P("tm", "space", None), P("tm", "space", None)),
        check_vma=False,
    )
```

```python
import functools
import jax
import jax.numpy as jnp
from jax import lax
from jax.experimental import pallas as pl
from jax.experimental.pallas import tpu as pltpu
from jax.sharding import PartitionSpec as P

STEPS = 4
GROUP = 4
SWEEPS = 2


DIFFUSION = 0.05
PAD = 8
CHUNK = 8
PIECES = 9
LANES = 128
MESH = pl.DeviceIdType.MESH


def block_of(rows):
    return max(size for size in range(8, min(rows, 32) + 1, 8) if rows % size == 0)


def kernel(
    points, strips, guess, kappa, rate, c_out, f_out,
    kw, rw, aw, ga, gb, x_ref, ya, yb, z_ref, w_ref, da, db, cr, vo, ve, vw, u1, u2, st,
    local_sem, k_send, k_recv, g_send, g_recv, c_send, c_recv, f_send, f_recv,
    t_send, t_recv, o_send, o_recv,
):
    rows, width = kappa.shape
    tiles = width // LANES
    half = rows // 2
    wide = ga.shape[1]
    full = vw.shape[1]
    halo = (wide - 2 * PAD - half) // 2
    margin = halo - 2 * STEPS
    chunks = (half + 2 * margin) // CHUNK
    skipped = margin // CHUNK
    kept = chunks - skipped
    pairs = points // 2
    tm, s = lax.axis_index("tm"), lax.axis_index("space")
    p, b = tm // 2, tm % 2
    coarse_scale = float(STEPS)
    shift = b * half
    partner = p * 2 + (1 - b)

    later, earlier = p < pairs - 1, p > 0
    below, above = s < strips - 1, s > 0
    even, odd = b == 0, b == 1

    targets = [
        (below, (tm, s + 1)), (above, (tm, s - 1)), (s >= 0, (partner, s)),
        (even & above, (tm + 1, s - 1)), (later, (tm + 2, s)),
        (odd & later & below, (tm + 1, s + 1)),
        (odd & later & above, (tm + 2, s - 1)),
    ]
    sources = [
        (below, (tm, s + 1)), (above, (tm, s - 1)), (s >= 0, (partner, s)),
        (odd & below, (tm - 1, s + 1)), (earlier, (tm - 2, s)),
        (even & earlier & above, (tm - 1, s - 1)),
        (odd & earlier & below, (tm - 2, s + 1)),
    ]
    barrier = pltpu.get_barrier_semaphore()
    for condition, device in sources:
        @pl.when(condition)
        def _(device=device):
            pl.semaphore_signal(barrier, inc=1, device_id=device, device_id_type=MESH)

    main = half + halo
    cut = PAD + (wide - 2 * PAD) // 16 * 8
    early = cut + 8 - PAD
    early_odd, late_odd = pl.ds(PAD, early), pl.ds(PAD + early, main - early)
    first, last = (0, halo), (rows - halo, halo)
    head = (0, main)
    tails = (rows - main, early), (rows - main + early, main - early)
    upper, lower = pl.ds(PAD, halo), pl.ds(PAD + main, halo)
    main_even = pl.ds(PAD + halo, main)
    end = pl.ds(PAD + halo + rows, halo)
    middle = pl.ds(PAD + halo, rows)
    own = guess.at[0]

    def columns(src, part):
        start, count = part
        return [src.at[pl.ds(start, count), pl.ds(t * LANES, LANES)] for t in range(tiles)]

    def fetch(src, part, dst, place, sem):
        def start():
            for t, column in enumerate(columns(src, part)):
                pltpu.make_async_copy(column, dst.at[t, place], sem).start()

        def wait():
            pltpu.make_async_copy(dst.at[:, place], dst.at[:, place], sem).wait()

        return start, wait

    def copy(src, dst, send, recv, device):
        return pltpu.make_async_remote_copy(
            src_ref=src, dst_ref=dst, send_sem=send, recv_sem=recv,
            device_id=device, device_id_type=MESH,
        )

    class Send:
        def __init__(self, src, part, dst, place, send, recv, device):
            self.start_all = [
                copy(column, dst.at[t, place], send, recv, device)
                for t, column in enumerate(columns(src, part))
            ]
            self.whole = copy(dst.at[:, place], dst.at[:, place], send, recv, device)

        def start(self):
            for one in self.start_all:
                one.start()

        def wait_recv(self):
            self.whole.wait_recv()

        def wait_send(self):
            self.whole.wait_send()

    k_local = fetch(kappa, (0, rows), kw, middle, local_sem.at[0])
    r_local = fetch(rate, (0, rows), rw, middle, local_sem.at[1])
    g_local = fetch(own, head, gb, main_even, local_sem.at[2])
    k_local[0]()
    r_local[0]()

    @pl.when(even)
    def _():
        g_local[0]()

    sends = [
        (below, Send(kappa, last, kw, upper, k_send.at[0], k_recv.at[0], (tm, s + 1))),
        (below, Send(rate, last, rw, upper, k_send.at[1], k_recv.at[1], (tm, s + 1))),
        (above, Send(kappa, first, kw, end, k_send.at[2], k_recv.at[2], (tm, s - 1))),
        (above, Send(rate, first, rw, end, k_send.at[3], k_recv.at[3], (tm, s - 1))),
        (even & below, Send(own, last, gb, upper, g_send.at[0], g_recv.at[0], (tm, s + 1))),
        (even & above, Send(own, first, gb, lower, g_send.at[1], g_recv.at[0], (tm + 1, s - 1))),
        (odd & later & below, Send(own, last, ga, upper, g_send.at[0], g_recv.at[2], (tm + 1, s + 1))),
        (odd & later & above, Send(own, first, ga, lower, g_send.at[1], g_recv.at[2], (tm + 2, s - 1))),
        (even, Send(own, tails[0], gb, early_odd, g_send.at[2], g_recv.at[1], (partner, s))),
        (odd & later, Send(own, tails[0], ga, early_odd, g_send.at[2], g_recv.at[3], (tm + 2, s))),
        (even, Send(own, tails[1], gb, late_odd, g_send.at[3], g_recv.at[4], (partner, s))),
        (odd & later, Send(own, tails[1], ga, late_odd, g_send.at[3], g_recv.at[5], (tm + 2, s))),
    ]
    piece = main // PIECES
    relays = [
        Send(own, (i * piece, piece), st, pl.ds(i * piece, piece), t_send.at[i], t_recv.at[i], (partner, s))
        for i in range(PIECES)
    ]
    onward = [
        copy(st.at[:, pl.ds(i * piece, piece)], ga.at[:, pl.ds(PAD + halo + i * piece, piece)],
             o_send.at[i], o_recv.at[i], (tm + 2, s))
        for i in range(PIECES)
    ]
    halves, fields = sends[:4], sends[4:]
    count = sum(condition.astype(jnp.int32) for condition, _ in targets)
    pl.semaphore_wait(barrier, count)
    for condition, transfer in sends:
        @pl.when(condition)
        def _(transfer=transfer):
            transfer.start()

    @pl.when(odd & later)
    def _():
        for relay in relays:
            relay.start()

    zeros = jnp.zeros((tiles, PAD, LANES), jnp.float32)
    for ref in (ga, gb, x_ref, ya, yb, z_ref, w_ref, cr, vo, vw, u1, u2):
        ref[:, pl.ds(0, PAD), :] = zeros
        ref[:, pl.ds(ref.shape[1] - PAD, PAD), :] = zeros
    rim = jnp.zeros((tiles, 2 * STEPS, LANES), jnp.float32)
    for ref in (cr, vo):
        ref[:, pl.ds(PAD, 2 * STEPS), :] = rim
        ref[:, pl.ds(wide - PAD - 2 * STEPS, 2 * STEPS), :] = rim
    blank = jnp.zeros((tiles, halo, LANES), jnp.float32)

    @pl.when(even & ~above)
    def _():
        ga[:, upper, :] = blank
        gb[:, upper, :] = blank

    @pl.when(odd & ~below)
    def _():
        ga[:, lower, :] = blank
        gb[:, lower, :] = blank

    @pl.when(~above)
    def _():
        kw[:, upper, :] = blank
        rw[:, upper, :] = blank

    @pl.when(~below)
    def _():
        kw[:, end, :] = blank
        rw[:, end, :] = blank

    k_local[1]()
    r_local[1]()

    @pl.when(above)
    def _():
        halves[0][1].wait_recv()
        halves[1][1].wait_recv()

    @pl.when(below)
    def _():
        halves[2][1].wait_recv()
        halves[3][1].wait_recv()

    def scaled(index, carry):
        part = pl.ds(pl.multiple_of(index * 32 + PAD, 8), 32)
        k = DIFFUSION * kw[:, part, :]
        kw[:, part, :] = k
        aw[:, part, :] = (1.0 + rw[:, part, :]) - 4.0 * k
        return carry

    lax.fori_loop(0, (rows + 2 * halo) // 32, scaled, 0)

    def step(src, low, size, offset, emit):
        lane = lax.broadcasted_iota(jnp.int32, (size, LANES), 1)
        at = pl.ds(pl.multiple_of(low + offset, 8), size)
        here = pl.ds(pl.multiple_of(low, 8), size)
        centre = src[0, here, :]
        before = after = 0.0
        to_left = pltpu.roll(centre, LANES - 1, 1)
        for t in range(tiles):
            to_right = pltpu.roll(centre, 1, 1)
            if t + 1 < tiles:
                following = src[t + 1, here, :]
                after = pltpu.roll(following, LANES - 1, 1)
            else:
                following, after = None, 0.0
            left = jnp.where(lane == 0, before, to_right)
            right = jnp.where(lane == LANES - 1, after, to_left)
            beside = src[t, pl.ds(low - 1, size), :] + src[t, pl.ds(low + 1, size), :]
            total = beside + (left + right)
            own_part = centre * (aw[t, at, :] - rw[t, at, :] * (centre * centre))
            emit(t, own_part + kw[t, at, :] * total, centre)
            before, centre, to_left = to_right, following, after

    def over(start, stop, act):
        size = block_of(stop - start)
        count = (stop - start) // size

        def body(index, carry):
            act(index * size + start, size)
            return carry

        lax.fori_loop(0, count, body, 0, unroll=True)

    def sweep(src, dst, start=PAD, stop=wide - PAD, offset=shift):
        def act(low, size):
            def emit(t, value, centre):
                dst[t, pl.ds(pl.multiple_of(low, 8), size), :] = value

            step(src, low, size, offset, emit)

        over(start, stop, act)

    def march(src, pair, dst, times, start, stop, keep):
        for turn in range(times):
            out = dst if turn == times - 1 else pair[turn % 2]
            sweep(src, out, keep if turn == times - 1 else start, stop)
            src = out

    def defects(field, relaxed, out, weight, start, stop, keep):
        march(field, (x_ref, z_ref), relaxed, STEPS, start, stop, keep)
        sweep(relaxed, w_ref, start, stop)
        march(w_ref, (z_ref, x_ref), x_ref, STEPS - 2, start, stop, start)

        def act(low, size):
            here = pl.ds(pl.multiple_of(low, 8), size)

            def emit(t, fine, centre):
                coarse = coarse_scale * w_ref[t, here, :] - (coarse_scale - 1.0) * relaxed[t, here, :]
                out[t, here, :] = fine - weight * coarse

            step(x_ref, low, size, shift, emit)

        over(keep, stop, act)

    early_rows = (PAD, cut, PAD)
    late_rows = (cut - 4 * STEPS, wide - PAD, cut - 2 * STEPS)
    needed = -(-(cut + 1 - PAD - halo) // piece)
    weight = jnp.where(p == 0, 0.0, 1.0)

    def relay_on(start, stop):
        @pl.when(even & later)
        def _():
            for i in range(start, stop):
                relays[i].wait_recv()
                onward[i].start()

    @pl.when(even)
    def _():
        g_local[1]()

    @pl.when(even & above)
    def _():
        fields[0][1].wait_recv()

    @pl.when(odd & below)
    def _():
        fields[1][1].wait_recv()

    @pl.when(odd)
    def _():
        fields[4][1].wait_recv()

    @pl.when(later)
    def _():
        defects(gb, yb, db, weight, *early_rows)

    relay_on(0, needed - 1)

    @pl.when(even & later)
    def _():
        defects(gb, yb, db, weight, *late_rows)

    relay_on(needed - 1, PIECES - 2)

    @pl.when(earlier)
    def _():
        @pl.when(even & above)
        def _():
            fields[2][1].wait_recv()

        @pl.when(odd & below)
        def _():
            fields[3][1].wait_recv()

        @pl.when(even)
        def _():
            for step_on in onward[:needed]:
                step_on.wait_recv()

        @pl.when(odd)
        def _():
            fields[5][1].wait_recv()

        defects(ga, ya, da, 1.0, *early_rows)

    relay_on(PIECES - 2, PIECES)

    @pl.when(odd)
    def _():
        fields[6][1].wait_recv()

    @pl.when(odd & later)
    def _():
        defects(gb, yb, db, weight, *late_rows)

    @pl.when(earlier)
    def _():
        @pl.when(even)
        def _():
            for step_on in onward[needed:]:
                step_on.wait_recv()

        @pl.when(odd)
        def _():
            fields[7][1].wait_recv()

        defects(ga, ya, da, 1.0, *late_rows)

    base = PAD + 2 * STEPS

    def chunk(index):
        return pl.ds(pl.multiple_of(index * CHUNK + base, 8), CHUNK)

    def chain(index):
        part = chunk(index)
        return copy(ve.at[:, part], cr.at[:, part], c_send.at[index], c_recv.at[index], (tm + 2, s))

    def target(index, side):
        return pl.ds(pl.multiple_of(index * CHUNK + PAD + side * half, 8), CHUNK)

    def forward(index, src):
        return copy(
            src.at[:, chunk(index)], vw.at[:, target(index, b)], f_send.at[index], f_recv.at[index],
            (partner, s),
        )

    def hand_over(index):
        @pl.when(even & (index < kept))
        def _():
            forward(index, vo).start()
            vw[:, target(index, 0), :] = cr[:, chunk(index), :]

        @pl.when(odd & (index >= skipped))
        def _():
            forward(index, cr).start()
            vw[:, target(index, 1), :] = vo[:, chunk(index), :]

    def corrected(src, defect, out, index):
        here = chunk(index)

        def emit(t, value, centre):
            image = coarse_scale * value - (coarse_scale - 1.0) * centre
            out[t, here, :] = image + defect[t, here, :]

        step(src, index * CHUNK + base, CHUNK, shift, emit)

    @pl.when(p == 0)
    def _():
        def body(index, carry):
            part = chunk(index)
            ve[:, part, :] = db[:, part, :]
            chain(index).start()
            vo[:, part, :] = yb[:, part, :]
            cr[:, part, :] = gb[:, part, :]
            hand_over(index)
            return carry

        lax.fori_loop(0, chunks, body, 0)

    @pl.when(earlier)
    def _():
        def body(index, carry):
            @pl.when(index < chunks)
            def _():
                chain(index).wait_recv()

            @pl.when((index >= 1) & (index <= chunks))
            def _():
                corrected(cr, da, vo, index - 1)

            @pl.when((index >= 2) & later)
            def _():
                corrected(vo, db, ve, index - 2)
                chain(index - 2).start()

            @pl.when((index >= 1) & (index <= chunks))
            def _():
                hand_over(index - 1)

            return carry

        lax.fori_loop(0, chunks + 2, body, 0)

    def collect(index, carry):
        forward(index + skipped * (1 - b), vo).wait_recv()
        return carry

    lax.fori_loop(0, kept, collect, 0)

    offset = halo - margin
    src = vw
    for turn in range(STEPS - 2):
        out = u1 if turn % 2 == 0 else u2
        sweep(src, out, PAD, full - PAD, offset)
        src = out

    def finish(low, size):
        out = pl.ds(pl.multiple_of(low - PAD - margin, 8), size)

        def emit(t, value, centre):
            lanes = pl.ds(t * LANES, LANES)
            f_out[0, out, lanes] = value
            c_out[0, out, lanes] = vw[t, pl.ds(pl.multiple_of(low, 8), size), :]

        step(src, low, size, offset, emit)

    over(PAD + margin, PAD + margin + rows, finish)

    for condition, transfer in sends:
        @pl.when(condition)
        def _(transfer=transfer):
            transfer.wait_send()

    @pl.when(later)
    def _():
        def body(index, carry):
            chain(index).wait_send()
            return carry

        lax.fori_loop(0, chunks, body, 0)

    @pl.when(odd & later)
    def _():
        for relay in relays:
            relay.wait_send()

    @pl.when(even & later)
    def _():
        for step_on in onward:
            step_on.wait_send()

    def sent(index, carry):
        forward(index + skipped * b, vo).wait_send()
        return carry

    lax.fori_loop(0, kept, sent, 0)


def halo_of(points):
    needed = 2 * STEPS + max(points - 3, 0) + STEPS - 1
    return -(-needed // CHUNK) * CHUNK


def chained(points, strips, guess, kappa, rate):
    rows, width = kappa.shape
    tiles = width // LANES
    halo = halo_of(points)
    margin = halo - 2 * STEPS
    wide = rows // 2 + 2 * halo + 2 * PAD
    full = rows + 2 * margin + 2 * PAD
    chunks = (rows // 2 + 2 * margin) // CHUNK
    f32 = jnp.float32

    def held(height):
        return pltpu.VMEM((tiles, height, LANES), f32)

    part, whole, coefficient = held(wide), held(full), held(rows + 2 * halo + 2 * PAD)
    dma = pltpu.SemaphoreType.DMA
    vmem = pl.BlockSpec(memory_space=pltpu.VMEM)
    anywhere = pl.BlockSpec(memory_space=pltpu.HBM)
    return pl.pallas_call(
        functools.partial(kernel, points, strips),
        out_shape=[jax.ShapeDtypeStruct(guess.shape, f32)] * 2,
        in_specs=[anywhere] * 3,
        out_specs=[vmem] * 2,
        scratch_shapes=[coefficient] * 3 + [part] * 12 + [whole] * 3 + [held(rows // 2 + halo)]
        + [dma((3,))] + [dma((4,))] * 3 + [dma((6,))] + [dma((chunks,))] * 4 + [dma((PIECES,))] * 4,
        compiler_params=pltpu.CompilerParams(
            collective_id=0, has_side_effects=True, vmem_limit_bytes=51 * 2**20
        ),
    )(guess, kappa, rate)


def extended(shard, sides, width):
    for axis, dim in sides:
        peers, length = (lax.axis_size(axis), shard.shape[dim])
        up = [(i, (i + 1) % peers) for i in range(peers - 1)]
        down = [(j, i) for i, j in up]
        last = lax.slice_in_dim(shard, length - width, length, axis=dim)
        initial = lax.slice_in_dim(shard, 0, width, axis=dim)
        before = lax.ppermute(last, axis, up)
        after = lax.ppermute(initial, axis, down)
        shard = jnp.concatenate([before, shard, after], axis=dim)
    return shard


def from_behind(value, axis, steps):
    count = lax.axis_size(axis)
    initial, last = (max(0, -steps), min(count, count - steps))
    return lax.ppermute(value, axis, [(source, source + steps) for source in range(initial, last)])


def advance_padded(padded, kappa, rate, scale):
    centre = padded[1:-1, 1:-1]
    laplace = (
        padded[2:, 1:-1] + padded[:-2, 1:-1] + padded[1:-1, 2:] + padded[1:-1, :-2] - 4.0 * centre
    )
    return centre + scale * (
        DIFFUSION * kappa * laplace + rate * (centre - centre * centre * centre)
    )


def deep_border(state, count):
    return extended(state, (("space", 0),), count)


def deep_step(wide, margin, widened, scale):
    rows = widened.shape[1] - 2 * STEPS
    height = wide.shape[0] - 2
    lower = STEPS - (margin - 1)
    kappa_rows = widened[0, lower : lower + height]
    rate_rows = widened[1, lower : lower + height]
    stepped = advance_padded(jnp.pad(wide, ((0, 0), (1, 1))), kappa_rows, rate_rows, scale)
    strip = lax.axis_index("space")
    total = rows * lax.axis_size("space")
    global_rows = strip * rows - (margin - 1) + lax.broadcasted_iota(jnp.int32, stepped.shape, 0)
    inside = (global_rows >= 0) & (global_rows < total)
    return jnp.where(inside, stepped, jnp.zeros_like(stepped))


def deep_march(wide, margin, widened, count):
    for repeat in range(count):
        wide = deep_step(wide, margin, widened, 1.0)
        margin = margin - 1
    return wide


def forward(state):
    return from_behind(state, "tm", 1)


def local(guess, kappa, rate):
    position = lax.axis_index("tm")
    member = position % GROUP
    coarse_scale = float(STEPS)
    state = guess[0]
    incoming = forward(state)
    widened = extended(jnp.stack([kappa, rate]), (("space", 1),), STEPS)
    marched = deep_march(deep_border(incoming, STEPS), STEPS, widened, STEPS)
    relaxed = jnp.where(position == 0, state, marched)
    incoming = forward(relaxed)
    wide = deep_border(incoming, STEPS)
    rows = relaxed.shape[0]
    band = jnp.pad(wide[STEPS - 1 : STEPS + rows + 1], ((0, 0), (1, 1)))
    coarse_image = advance_padded(band, kappa, rate, coarse_scale)
    fine_image = deep_march(wide, STEPS, widened, STEPS)
    defect = jnp.where(position == 0, jnp.zeros_like(fine_image), fine_image - coarse_image)
    coarse = relaxed
    for sweep_number in range(SWEEPS):
        for turn in range(GROUP):
            arrived = from_behind(coarse, "tm", 1)
            framed = extended(arrived, (("space", 0),), 1)
            framed = jnp.pad(framed, ((0, 0), (1, 1)))
            updated = advance_padded(framed, kappa, rate, coarse_scale) + defect
            if turn + 1 < GROUP:
                active = member == turn + 1
            else:
                active = (member == 0) & (position >= GROUP)
            coarse = jnp.where(active, updated, coarse)
    last_fine = deep_march(deep_border(coarse, STEPS - 1), STEPS - 1, widened, STEPS - 1)
    return (coarse[None], last_fine[None])


def solution(mesh):
    points, strips = mesh.shape["tm"], mesh.shape["space"]

    def run(guess, kappa, rate):
        rows, width = kappa.shape
        settled = points <= GROUP * SWEEPS and points % 2 == 0 and points >= 4
        aligned = rows % 32 == 0 and width % LANES == 0 and (2 * STEPS) % 8 == 0
        if settled and aligned and halo_of(points) % 16 == 0 and (rows // 2 + halo_of(points)) % (8 * PIECES) == 0 and 2 * halo_of(points) <= rows:
            return tuple(chained(points, strips, guess, kappa, rate))
        return local(guess, kappa, rate)

    return jax.shard_map(
        run,
        mesh=mesh,
        in_specs=(P("tm", "space", None), P("space", None), P("space", None)),
        out_specs=(P("tm", "space", None), P("tm", "space", None)),
        check_vma=False,
    )
```
